256 devices in a mesh: leaf: 16 (over z, core), front: 16 (over x, y).
Axes of the slice: x: 4, y: 4, z: 8, core: 2. Of those that a mesh axis runs over, the one named last changes fastest.
Arguments:
- right_side_0: bfloat16 [16, 16, 256, 128], P('leaf', 'front'), may hold values from -6 to 6
- right_side_1: bfloat16 [16, 16, 128, 128], P('leaf', 'front'), may hold values from -6 to 6
- right_side_2: bfloat16 [16, 16, 64, 128], P('leaf', 'front'), may hold values from -6 to 6
- right_side_3: bfloat16 [16, 16, 32, 128], P('leaf', 'front'), may hold values from -6 to 6
- right_side_4: bfloat16 [16, 16, 16, 128], P('leaf', 'front'), may hold values from -6 to 6
- inverse_0: bfloat16 [16, 16, 256, 4096], P('leaf', 'front'), as said below
- inverse_1: bfloat16 [16, 16, 128, 4096], P('leaf', 'front'), as said below
- inverse_2: bfloat16 [16, 16, 64, 4096], P('leaf', 'front'), as said below
- inverse_3: bfloat16 [16, 16, 32, 4096], P('leaf', 'front'), as said below
- inverse_4: bfloat16 [16, 16, 16, 4096], P('leaf', 'front'), as said below
- lower_0: bfloat16 [16, 16, 256, 2048], P('leaf', 'front'), may hold values from -0.0625 to 0.0625
- lower_1: bfloat16 [16, 16, 128, 2048], P('leaf', 'front'), may hold values from -0.0625 to 0.0625
- lower_2: bfloat16 [16, 16, 64, 2048], P('leaf', 'front'), may hold values from -0.0625 to 0.0625
- lower_3: bfloat16 [16, 16, 32, 2048], P('leaf', 'front'), may hold values from -0.0625 to 0.0625
- block_map_0: int32 [16, 16], replicated, may hold values from 0 to 47, as said below
- block_map_1: int32 [8, 16], replicated, may hold values from 0 to 47, as said below
- block_map_2: int32 [4, 16], replicated, may hold values from 0 to 47, as said below
- block_map_3: int32 [2, 16], replicated, may hold values from 0 to 31, as said below
Outputs:
- solution_0: float32 [16, 16, 256, 128], P('leaf', 'front')
- solution_1: float32 [16, 16, 128, 128], P('leaf', 'front')
- solution_2: float32 [16, 16, 64, 128], P('leaf', 'front')
- solution_3: float32 [16, 16, 32, 128], P('leaf', 'front')
- solution_4: float32 [16, 16, 16, 128], P('leaf', 'front')
The draws below stay inside these ranges and needn't reach their ends.
Inputs may be any that keep to these rules, and one draw needn't show every extreme that they name: `inverse_0`: each front's pivot inverse is lower triangular, with its diagonal between 0.8 and 1.2. `inverse_1`: as for inverse_0. `inverse_2`: as for inverse_0. `inverse_3`: as for inverse_0. `inverse_4`: as for inverse_0. `block_map_0`: each row's entries are all different and increasing; the last entry of every row is the parent's last block. `block_map_1`: as for block_map_0. `block_map_2`: as for block_map_0. `block_map_3`: as for block_map_0, into the root's pivot blocks.
All inputs are finite; a program needn't handle non-finite values.
Results may differ from the reference program's by a relative error of at most 0.033.
Values may be sent and summed in bfloat16 or wider, within the bound.
A program may use at most 128 MiB of HBM per device.

```python
import jax
import jax.numpy as jnp
from jax import lax

P_SIZE = 4096
C = 2048
R = 128
BLOCK = 128
FRONTS = 16
CELLS = 16


def inverse_block(key, height):
    rows_cell = P_SIZE // (CELLS * 2 ** height)
    shape = (FRONTS, CELLS, rows_cell, P_SIZE)
    noise = jnp.clip(jax.random.normal(key, shape, jnp.float32), -6.0, 6.0)
    pivot = jax.random.uniform(jax.random.fold_in(key, 7), shape, jnp.float32, 0.8, 1.2)
    slab = lax.broadcasted_iota(jnp.int32, shape, 0) % 2 ** height
    cell = lax.broadcasted_iota(jnp.int32, shape, 1)
    inner = lax.broadcasted_iota(jnp.int32, shape, 2)
    column = lax.broadcasted_iota(jnp.int32, shape, 3)
    row_number = (slab * CELLS + cell) * rows_cell + inner
    strict = noise * (0.7 / P_SIZE ** 0.5)
    values = jnp.where(column < row_number, strict, jnp.where(column == row_number, pivot, 0.0))
    return values.astype(jnp.bfloat16)


def block_rows(key, height, count):
    fronts = FRONTS // 2 ** height
    picks = C // BLOCK
    keys = jax.random.split(key, fronts)

    def single(front_key):
        order = jax.random.permutation(front_key, count - 1)[:picks - 1]
        return jnp.concatenate([jnp.sort(order).astype(jnp.int32), jnp.full((1,), count - 1, jnp.int32)])
    return jax.vmap(single)(keys).astype(jnp.int32)


def draw_inverse_0(key, part):
    key = jax.random.fold_in(key, 11)
    return inverse_block(key, 0)


def draw_inverse_1(key, part):
    key = jax.random.fold_in(key, 12)
    return inverse_block(key, 1)


def draw_inverse_2(key, part):
    key = jax.random.fold_in(key, 13)
    return inverse_block(key, 2)


def draw_inverse_3(key, part):
    key = jax.random.fold_in(key, 14)
    return inverse_block(key, 3)


def draw_inverse_4(key, part):
    key = jax.random.fold_in(key, 15)
    return inverse_block(key, 4)


def draw_block_map_0(key, part):
    key = jax.random.fold_in(key, 21)
    return block_rows(key, 0, (P_SIZE + C) // BLOCK)


def draw_block_map_1(key, part):
    key = jax.random.fold_in(key, 22)
    return block_rows(key, 1, (P_SIZE + C) // BLOCK)


def draw_block_map_2(key, part):
    key = jax.random.fold_in(key, 23)
    return block_rows(key, 2, (P_SIZE + C) // BLOCK)


def draw_block_map_3(key, part):
    key = jax.random.fold_in(key, 24)
    return block_rows(key, 3, P_SIZE // BLOCK)


def steps_of(key, extent, cuts, least, largest):
    gain = 1.0
    for position, blocks in cuts:
        steps = jax.random.uniform(jax.random.fold_in(jax.random.fold_in(key, 6), position), (blocks,), jnp.float32, least / len(cuts), largest / len(cuts))
        gain = gain * jnp.repeat(jnp.exp(steps), extent[position] // blocks).reshape((-1,) + (1,) * (len(extent) - 1 - position))
    return gain


def centred(stream_key, extent, scale, bound, cuts=(), held_as=jnp.bfloat16):
    entries = jax.random.normal(stream_key, extent, jnp.float32) * scale
    if len(cuts) > 0:
        entries = steps_of(stream_key, extent, cuts, -0.22, 0.18) * entries
    return jnp.clip(entries, min=-bound, max=bound).astype(held_as)


def setup_inputs(seed: int = 0) -> dict:
    splits = jax.random.split(jax.random.key(seed), 19)
    right_side_0 = centred(splits[0], (FRONTS, CELLS, P_SIZE // CELLS, R), 1.0, 6.0, ((0, 16), (1, 16)))
    right_side_1 = centred(splits[1], (FRONTS, CELLS, P_SIZE // (CELLS * 2), R), 1.0, 6.0, ((0, 16), (1, 16)))
    right_side_2 = centred(splits[2], (FRONTS, CELLS, P_SIZE // (CELLS * 4), R), 1.0, 6.0, ((0, 16), (1, 16)))
    right_side_3 = centred(splits[3], (FRONTS, CELLS, P_SIZE // (CELLS * 8), R), 1.0, 6.0, ((0, 16), (1, 16)))
    right_side_4 = centred(splits[4], (FRONTS, CELLS, P_SIZE // (CELLS * 16), R), 1.0, 6.0, ((0, 16), (1, 16)))
    inverse_0 = draw_inverse_0(jax.random.fold_in(splits[18], 71), 0)
    inverse_1 = draw_inverse_1(jax.random.fold_in(splits[18], 71), 0)
    inverse_2 = draw_inverse_2(jax.random.fold_in(splits[18], 71), 0)
    inverse_3 = draw_inverse_3(jax.random.fold_in(splits[18], 71), 0)
    inverse_4 = draw_inverse_4(jax.random.fold_in(splits[18], 71), 0)
    lower_0 = centred(splits[10], (FRONTS, CELLS, P_SIZE // CELLS, C), (2 * P_SIZE) ** -0.5, 0.0625, ((0, 16), (1, 16)))
    lower_1 = centred(splits[11], (FRONTS, CELLS, P_SIZE // (CELLS * 2), C), (2 * P_SIZE) ** -0.5, 0.0625, ((0, 16), (1, 16)))
    lower_2 = centred(splits[12], (FRONTS, CELLS, P_SIZE // (CELLS * 4), C), (2 * P_SIZE) ** -0.5, 0.0625, ((0, 16), (1, 16)))
    lower_3 = centred(splits[13], (FRONTS, CELLS, P_SIZE // (CELLS * 8), C), (2 * P_SIZE) ** -0.5, 0.0625, ((0, 16), (1, 16)))
    block_map_0 = draw_block_map_0(jax.random.fold_in(splits[18], 71), 0)
    block_map_1 = draw_block_map_1(jax.random.fold_in(splits[18], 71), 0)
    block_map_2 = draw_block_map_2(jax.random.fold_in(splits[18], 71), 0)
    block_map_3 = draw_block_map_3(jax.random.fold_in(splits[18], 71), 0)
    return dict(right_side_0=right_side_0, right_side_1=right_side_1, right_side_2=right_side_2, right_side_3=right_side_3, right_side_4=right_side_4, inverse_0=inverse_0, inverse_1=inverse_1, inverse_2=inverse_2, inverse_3=inverse_3, inverse_4=inverse_4, lower_0=lower_0, lower_1=lower_1, lower_2=lower_2, lower_3=lower_3, block_map_0=block_map_0, block_map_1=block_map_1, block_map_2=block_map_2, block_map_3=block_map_3)


def by_front(array, height):
    count = array.shape[0] // 2 ** height
    return array.reshape(count, -1, array.shape[-1])


def assemble(pieces, block_map, blocks_total):
    parents = pieces.shape[0] // 2
    width = pieces.shape[-1]
    blocks = pieces.reshape(parents, 2 * (C // BLOCK), BLOCK, width).astype(jnp.float32)
    targets = block_map.reshape(parents, -1)

    def place(content, where):
        return jnp.zeros((blocks_total, BLOCK, width), jnp.float32).at[where].add(content)

    placed = jax.vmap(place)(blocks, targets)
    return placed.reshape(parents, blocks_total * BLOCK, width)


def pick_blocks(table, where):
    return table[where]


def reference(right_side_0, right_side_1, right_side_2, right_side_3, right_side_4,
              inverse_0, inverse_1, inverse_2, inverse_3, inverse_4,
              lower_0, lower_1, lower_2, lower_3,
              block_map_0, block_map_1, block_map_2, block_map_3):
    sides = [by_front(a, h) for h, a in enumerate([right_side_0, right_side_1, right_side_2, right_side_3, right_side_4])]
    inverses = [by_front(a, h) for h, a in enumerate([inverse_0, inverse_1, inverse_2, inverse_3, inverse_4])]
    lowers = [by_front(a, h) for h, a in enumerate([lower_0, lower_1, lower_2, lower_3])]
    block_maps = [block_map_0, block_map_1, block_map_2, block_map_3]
    width = right_side_0.shape[-1]
    upward = []
    assembled = None
    for height in range(5):
        count = FRONTS // 2 ** height
        if height == 0:
            pivot_part = jnp.zeros((count, P_SIZE, width), jnp.float32)
        else:
            pivot_part = assembled[:, :P_SIZE]
        right = (sides[height].astype(jnp.float32) - pivot_part).astype(jnp.bfloat16)
        solved = jnp.stack([jnp.dot(inverses[height][j], right[j], preferred_element_type=jnp.float32)
                            for j in range(count)]).astype(jnp.bfloat16)
        upward.append(solved)
        if height < 4:
            update = jnp.stack([jnp.dot(lowers[height][j].T, solved[j], preferred_element_type=jnp.float32)
                                for j in range(count)])
            if height > 0:
                update = update + assembled[:, P_SIZE:]
            update = update.astype(jnp.bfloat16)
            blocks_total = (P_SIZE + C) // BLOCK if height < 3 else P_SIZE // BLOCK
            assembled = assemble(update, block_maps[height], blocks_total)
    results = [None] * 5
    parent = None
    gathered = None
    for height in (4, 3, 2, 1, 0):
        count = FRONTS // 2 ** height
        if height == 4:
            adjusted = upward[4]
        else:
            expanded = jnp.repeat(parent, 2, axis=0)[:count]
            blocks = expanded.reshape(count, -1, BLOCK, width)
            gathered = jax.vmap(pick_blocks)(blocks, block_maps[height]).reshape(count, C, width)
            reaction = jnp.stack([jnp.dot(lowers[height][j], gathered[j], preferred_element_type=jnp.float32)
                                  for j in range(count)])
            adjusted = (upward[height].astype(jnp.float32) - reaction).astype(jnp.bfloat16)
        solution = jnp.stack([jnp.dot(inverses[height][j].T, adjusted[j], preferred_element_type=jnp.float32)
                              for j in range(count)])
        results[height] = solution.reshape(FRONTS, CELLS, -1, width)
        if height > 0:
            rounded = solution.astype(jnp.bfloat16)
            parent = rounded if height == 4 else jnp.concatenate([rounded, gathered], axis=1)
    return (results[0], results[1], results[2], results[3], results[4])
```

```python
import types

import jax
import jax.numpy as jnp
from jax import lax
from jax.experimental import pallas as pl
from jax.experimental.pallas import tpu as pltpu
from jax.sharding import PartitionSpec as P

MESH = pl.DeviceIdType.MESH
BF = jnp.bfloat16
F32 = jnp.float32
NT = (((1,), (1,)), ((), ()))
NN = (((1,), (0,)), ((), ()))
FRONT = 16
LEVELS = range(5)


def packed(numbers):
    return sum(n << 2 * i for i, n in enumerate(numbers))


STEPS = sorted(((dx, dy) for dx in range(4) for dy in range(4)),
               key=lambda s: -min(s[0], 4 - s[0]) - min(s[1], 4 - s[1]))
STEPS_X = packed(s[0] for s in STEPS[:15])
STEPS_Y = packed(s[1] for s in STEPS[:15])


def dot(a, b, dims):
    return lax.dot_general(a, b, dims, preferred_element_type=F32)


def side_by_side(parts):
    return jnp.concatenate(list(parts), axis=1)


def scratch_shapes():
    dma = pltpu.SemaphoreType.DMA

    def vm(*shape, dtype=BF):
        return pltpu.VMEM(shape, dtype)

    def per(make, levels):
        return [make(h) if h in levels else None for h in LEVELS]

    t = types.SimpleNamespace()
    low, high, every, lowered = range(0, 1), range(1, 5), range(0, 5), range(1, 4)
    t.v = per(lambda h: vm(256, 4096), every)
    t.u = per(lambda h: vm(256, 2048), range(0, 4))
    t.vblk = per(lambda h: vm(33, 256, 128), high)
    t.v_load = per(lambda h: dma(()), every)
    t.u_load = per(lambda h: dma(()), range(0, 4))
    t.v_send = per(lambda h: dma(()), range(2, 5))
    t.u_send = per(lambda h: dma(()), range(2, 4))
    t.v_fwd = per(lambda h: dma((2,)), high)
    t.u_fwd = per(lambda h: dma((2,)), lowered)
    t.side = vm(256, 128)
    t.side_load = dma(())
    t.r = vm(32, 128, 128)
    t.r_send = dma((16,))
    t.r_recv = dma((16,))
    t.zb = per(lambda h: vm(128, 128), range(2, 5))
    t.zb_send = per(lambda h: dma(()), range(2, 5))
    t.zb_recv = per(lambda h: dma(()), range(2, 5))
    t.bn = per(lambda h: vm(128, 128), high)
    t.bn_send = per(lambda h: dma(()), high)
    t.bn_recv = per(lambda h: dma(()), high)
    t.bh = per(lambda h: vm(2, 64, 128), high)
    t.b = per(lambda h: vm(32, 64, 128), high)
    t.b_swap = per(lambda h: dma((2,)), high)
    t.b_send = per(lambda h: dma(()), high)
    t.b_recv = per(lambda h: dma(()), high)
    t.up_out = per(lambda h: vm(16, 128 if h == 0 else 64, 128), range(0, 4))
    t.up_in = per(lambda h: vm(15, 128 if h == 0 else 64, 128), range(0, 4))
    t.up_send = per(lambda h: dma(()), range(0, 4))
    t.up_recv = per(lambda h: dma(()), range(0, 4))
    t.halves = vm(2, 64, 128)
    t.vb = per(lambda h: vm(2, 17, 64, 128), high)
    t.swap = per(lambda h: dma((2,)), high)
    t.vb_send = per(lambda h: dma(()), high)
    t.vb_recv = per(lambda h: dma((2, 16)), high)
    t.y = per(lambda h: vm(128 if h == 0 else 64, 256, dtype=F32), every)
    t.w = per(lambda h: vm(64, 256), high)
    t.sel_out = per(lambda h: vm(16, 128 if h == 1 else 64, 128), high)
    t.sel_in = per(lambda h: vm(15, 128 if h == 1 else 64, 128), high)
    t.sel_send = per(lambda h: dma(()), high)
    t.sel_recv = per(lambda h: dma(()), high)
    t.g_half = vm(2, 64, 128)
    t.g_swap = dma((2,))
    t.g = per(lambda h: vm(16, 128, 128) if h == 0 else vm(17, 64, 128), range(0, 4))
    t.g_send = per(lambda h: dma(()), range(0, 4))
    t.g_recv = per(lambda h: dma((16,)), range(0, 4))
    t.x_out = per(lambda h: vm(2, 16, 64, 128), high)
    t.x_in = per(lambda h: vm(15, 2, 64, 128), high)
    t.x_send = per(lambda h: dma(()), high)
    t.x_recv = per(lambda h: dma(()), high)
    t.x_sum = per(lambda h: vm(2, 64, 128, dtype=F32), high)
    t.x_full = per(lambda h: vm(2, 64, 128, dtype=F32), high)
    t.x_rows = per(lambda h: vm(128, 128, dtype=F32), high)
    t.xx = per(lambda h: dma((2,)), high)
    t.x0_out = vm(16, 2, 128, 128)
    t.x0_in = vm(16, 2, 128, 128)
    t.x0_sum = vm(2, 128, 128, dtype=F32)
    t.x0_send = dma((16,))
    t.x0_recv = dma((16,))
    return t


def flat(t):
    out = []
    for entry in vars(t).values():
        out += [e for e in entry if e is not None] if isinstance(entry, list) else [entry]
    return out


def unflat(t, refs):
    refs = iter(refs)
    s = types.SimpleNamespace()
    for name, entry in vars(t).items():
        if isinstance(entry, list):
            vars(s)[name] = [None if e is None else next(refs) for e in entry]
        else:
            vars(s)[name] = next(refs)
    return s


def kernel(*refs):
    sides = refs[0:5]
    invs = refs[5:10]
    lows = refs[10:14]
    maps = refs[14:18]
    out = refs[18]
    s = unflat(scratch_shapes(), refs[19:])

    leaf = lax.axis_index("leaf")
    f = lax.axis_index("front")
    z = leaf // 2
    c = leaf % 2
    other = 1 - c

    def dev(z_, c_, f_):
        return (2 * z_ + c_, f_)

    def remote(src, dst, send, recv, device):
        return pltpu.make_async_remote_copy(
            src_ref=src, dst_ref=dst, send_sem=send, recv_sem=recv,
            device_id=device, device_id_type=MESH)

    def wait(ref, sem):
        pltpu.make_async_copy(ref, ref, sem).wait()

    def loop(lo, hi, body):
        lax.fori_loop(lo, hi, lambda i, carry: (body(i), carry)[1], 0)

    fx, fy = f // 4, f % 4

    def step_of(k):
        if isinstance(k, int):
            return STEPS[k]
        return (STEPS_X >> 2 * k) % 4, (STEPS_Y >> 2 * k) % 4

    def plane(k):
        dx, dy = step_of(k)
        return (fx + dx) % 4 * 4 + (fy + dy) % 4

    def source(k):
        dx, dy = step_of(k)
        return (fx + 4 - dx) % 4 * 4 + (fy + 4 - dy) % 4

    def group(h):
        n = 2 ** (h - 1)
        zrel = z % n
        return n, zrel, z - zrel

    def own(ref):
        return ref.at[0, 0]

    def rows(first, count):
        return pl.ds(pl.multiple_of(first, count), count)

    def columns(ref, block, count=1):
        return ref[:, pl.ds(pl.multiple_of(block * 128, 128 * count), 128 * count)]

    side_copy = pltpu.make_async_copy(own(sides[0]), s.side, s.side_load)
    side_copy.start()
    barrier = pltpu.get_barrier_semaphore()

    def greet_plane(d):
        q = (c * FRONT + f + d) % (2 * FRONT)
        pl.semaphore_signal(barrier, inc=1, device_id=dev(z, q // FRONT, q % FRONT),
                            device_id_type=MESH)

    def greet_line(d):
        pl.semaphore_signal(barrier, inc=1, device_id=dev((z + d) % 8, c, f),
                            device_id_type=MESH)

    loop(1, 2 * FRONT, greet_plane)
    loop(1, 8, greet_line)
    load_v0 = pltpu.make_async_copy(own(invs[0]), s.v[0], s.v_load[0])
    load_u0 = pltpu.make_async_copy(own(lows[0]), s.u[0], s.u_load[0])
    load_v0.start()
    load_u0.start()
    for h in range(1, 5):
        n, zrel, _ = group(h)
        m = 256 >> h
        at = rows(c * 128 + zrel * m, m)
        pltpu.make_async_copy(own(invs[h]), s.v[h].at[at], s.v_load[h]).start()
        if h < 4:
            pltpu.make_async_copy(own(lows[h]), s.u[h].at[at], s.u_load[h]).start()
        if h > 1:
            pltpu.make_async_copy(own(sides[h]), s.zb[h].at[rows(zrel * m, m)], s.zb_recv[h]).start()
    side_copy.wait()
    for k in range(2):
        s.r[2 * f + k] = s.side[k * 128:(k + 1) * 128, :].astype(F32).T.astype(BF)
    for h in range(1, 5):
        s.vb[h][0, 16] = jnp.zeros((64, 128), BF)
        s.vb[h][1, 16] = jnp.zeros((64, 128), BF)
        s.vblk[h][32] = jnp.zeros((256, 128), BF)
        if h < 4:
            s.g[h][16] = jnp.zeros((64, 128), BF)
    pl.semaphore_wait(barrier, 31 + 7)

    def send_b0(k):
        to = plane(k)

        @pl.when(to > f)
        def _():
            mine = s.r.at[pl.ds(2 * f, 2)]
            remote(mine, mine, s.r_send.at[to], s.r_recv.at[f], dev(z, c, to)).start()

    loop(0, 15, send_b0)

    def block_owner(h, zr):
        n = 2 ** (h - 1)
        m = 256 >> h
        p = (2 * zr + c) * (32 >> h) + f // n
        return p % 2, p // 2, (f % n) * m

    def send_block_rows(h, src, zr):
        m = 256 >> h
        co, fo, row = block_owner(h, zr)
        dst = s.bn[h].at[rows(row, m)]
        here = jnp.logical_and(co == c, fo == f)

        @pl.when(here)
        def _():
            pltpu.make_async_copy(src, dst, s.bn_recv[h]).start()

        @pl.when(jnp.logical_not(here))
        def _():
            remote(src, dst, s.bn_send[h], s.bn_recv[h], dev(z, co, fo)).start()

    def gather_factor(h, ref, mine, send, load):
        n, zrel, zbase = group(h)
        m = 256 >> h
        dst = ref.at[rows(c * 128 + zrel * m, m)]
        for d in range(1, n):
            remote(own(mine), dst, send, load, dev(zbase + (zrel + d) % n, c, f)).start()

    def gather_level(h):
        gather_factor(h, s.v[h], invs[h], s.v_send[h], s.v_load[h])
        if h < 4:
            gather_factor(h, s.u[h], lows[h], s.u_send[h], s.u_load[h])

    def forward_factor(ref, load, fwd):
        part = ref.at[rows(c * 128, 128)]
        wait(part, load)
        remote(part, part, fwd.at[0], fwd.at[1], dev(z, other, f)).start()

    def forward_level(h):
        forward_factor(s.v[h], s.v_load[h], s.v_fwd[h])
        if h < 4:
            forward_factor(s.u[h], s.u_load[h], s.u_fwd[h])

    def have_forward(ref, fwd):
        wait(ref.at[rows(other * 128, 128)], fwd.at[1])

    send_block_rows(1, own(sides[1]), 0)
    for h in range(2, 5):
        n, zrel, zbase = group(h)
        m = 256 >> h
        for d in range(1, n):
            remote(own(sides[h]), s.zb[h].at[rows(zrel * m, m)], s.zb_send[h], s.zb_recv[h],
                   dev(zbase + (zrel + d) % n, c, f)).start()
    gather_level(2)
    forward_level(1)

    load_v0.wait()

    def y0_term(k):
        return dot(side_by_side([s.r[2 * k], s.r[2 * k + 1]]), columns(s.v[0], 2 * k, 2), NT)

    def y0_step(d, acc):
        k = f - d
        wait(s.r.at[pl.ds(0, 2)], s.r_recv.at[k])
        return acc + y0_term(k)

    y0 = lax.fori_loop(1, f + 1, y0_step, y0_term(f))
    s.y[0][...] = y0
    y0 = y0.astype(BF)
    load_u0.wait()

    def by_fours(body):
        loop(0, 3, lambda q: body([4 * q, 4 * q + 1, 4 * q + 2, 4 * q + 3]))
        body([12, 13, 14, 15])

    def here(k):
        return isinstance(k, int) and k == 15

    def up(h, y):
        def four(ks):
            part = dot(y, side_by_side(columns(s.u[h], plane(k)) for k in ks), NN).astype(BF)
            for n, k in enumerate(ks):
                i = plane(k)
                s.up_out[h][i] = part[:, n * 128:(n + 1) * 128]
                if not here(k):
                    remote(s.up_out[h].at[i], s.up_in[h].at[k], s.up_send[h], s.up_recv[h],
                           dev(z, c, i)).start()

        by_fours(four)

    up(0, y0)

    def turn_b(h):
        wait(s.bn[h], s.bn_recv[h])
        turned = s.bn[h][...].astype(F32).T.astype(BF)
        s.bh[h][0] = turned[:64]
        s.bh[h][1] = turned[64:]
        block = 2 * f + c
        s.b[h][block] = s.bh[h][c]
        remote(s.bh[h].at[other], s.b[h].at[block], s.b_swap[h].at[0], s.b_swap[h].at[1],
               dev(z, other, f)).start()

    def spread_b(h):
        wait(s.b[h].at[0], s.b_swap[h].at[1])
        both = s.b[h].at[pl.ds(2 * f, 2)]
        loop(0, 15, lambda k: remote(both, both, s.b_send[h], s.b_recv[h],
                                     dev(z, c, plane(k))).start())

    def split_columns(h):
        have_forward(s.v[h], s.v_fwd[h])

        def one(k):
            s.vblk[h][k] = columns(s.v[h], k)

        loop(0, 32, one)

    turn_b(1)
    for h in range(2, 5):
        m = 256 >> h
        wait(s.zb[h], s.zb_recv[h])
        for zr in range(2 ** (h - 1)):
            send_block_rows(h, s.zb[h].at[pl.ds(zr * m, m)], zr)
    gather_level(3)
    split_columns(1)
    spread_b(1)

    def send_child(h, child, kind):
        at = s.vb[h].at[child, f]
        loop(0, 15, lambda k: remote(at, at, s.vb_send[h], s.vb_recv[h].at[kind, f],
                                     dev(z, c, plane(k))).start())

    def side_term(h):
        wait(s.b[h].at[pl.ds(0, 30)], s.b_recv[h])

        def step(j, acc):
            part = side_by_side(s.b[h][8 * j + k] for k in range(8))
            return acc + dot(part, columns(s.v[h], 8 * j, 8), NT)

        return lax.fori_loop(0, 4, step, jnp.zeros((64, 256), F32))

    def child_term(h, child, kind, acc):
        table = maps[h - 1]
        row = 2 * (z // 2 ** (h - 1)) + child

        def pair(ks):
            at = [jnp.minimum(table[row, k], 32) for k in ks]
            return dot(side_by_side(s.vb[h][child, k] for k in ks),
                       side_by_side(s.vblk[h][a] for a in at), NT)

        def arrived(k):
            wait(s.vb[h].at[0, 0], s.vb_recv[h].at[kind, source(k)])

        def step(q, acc):
            arrived(14 - 2 * q)
            arrived(13 - 2 * q)
            return acc - pair([source(14 - 2 * q), source(13 - 2 * q)])

        acc = lax.fori_loop(0, 7, step, acc)
        arrived(0)
        return acc - pair([f, source(0)])

    def bottom_block(h, child):
        table = maps[h - 1]
        row = 2 * (z // 2 ** (h - 1)) + child
        less = jnp.int32(0)
        hit = jnp.int32(0)
        for i in range(16):
            less = less + (table[row, i] < 32 + f).astype(jnp.int32)
            hit = hit + (table[row, i] == 32 + f).astype(jnp.int32)
        return jnp.where(hit > 0, less, 16)

    def summed(ref, first):
        total = first
        for k in range(15):
            total = total + ref[k].astype(F32)
        return total

    def give_blocks(h, mine, half, sibling):
        remote(half, s.vb[h].at[mine, f], s.swap[h].at[0], s.swap[h].at[1], sibling).start()
        send_child(h, mine, 0)
        wait(s.vb[h].at[mine, f], s.swap[h].at[1])
        send_child(h, 1 - mine, 1)

    wait(s.up_in[0], s.up_recv[0])
    total = summed(s.up_in[0], s.up_out[0][f].astype(F32)).astype(BF)
    s.halves[0] = total[:64]
    s.halves[1] = total[64:]
    s.vb[1][c, f] = s.halves[c]
    give_blocks(1, c, s.halves.at[other], dev(z, other, f))
    for h in range(2, 5):
        turn_b(h)

    for h in range(1, 5):
        mine = c if h == 1 else z // 2 ** (h - 2) % 2
        acc = side_term(h)
        acc = child_term(h, mine, 0, acc)
        acc = child_term(h, 1 - mine, 1, acc)
        s.y[h][...] = acc
        y = acc.astype(BF)
        if h == 4:
            s.w[4][...] = y
            break
        have_forward(s.u[h], s.u_fwd[h])
        up(h, y)
        spread_b(h + 1)
        forward_level(h + 1)
        bottom = [bottom_block(h, child) for child in range(2)]
        split_columns(h + 1)
        kept = s.vb[h][0, bottom[0]].astype(F32) + s.vb[h][1, bottom[1]].astype(F32)
        kept = kept + s.up_out[h][f].astype(F32)
        wait(s.up_in[h], s.up_recv[h])
        step = 2 ** (h - 1)
        mine = z // step % 2
        s.vb[h + 1][mine, f] = summed(s.up_in[h], kept).astype(BF)
        give_blocks(h + 1, mine, s.vb[h + 1].at[mine, f], dev(z + step - 2 * step * mine, c, f))
        if h == 1:
            gather_level(4)

    def take_x(h):
        wait(s.x_in[h], s.x_recv[h])
        n = 2 ** (h - 1)
        s.x_sum[h][...] = summed(s.x_in[h], s.x_out[h][:, f // n].astype(F32))
        s.x_full[h][c] = s.x_sum[h][c]
        remote(s.x_sum[h].at[other], s.x_full[h].at[c], s.xx[h].at[0], s.xx[h].at[1],
               dev(z, other, f)).start()

    def give_x(h):
        wait(s.x_full[h].at[0], s.xx[h].at[1])
        n = 2 ** (h - 1)
        m = 256 >> h
        s.x_rows[h][...] = s.x_full[h][...].reshape(128, 128).T
        out[m:2 * m, :] = s.x_rows[h][rows((f % n) * m, m), :]

    def reaction(h):
        def pair(ks):
            return dot(side_by_side(s.g[h][k] for k in ks),
                       side_by_side(columns(s.u[h], k) for k in ks), NT)

        def arrived(k):
            wait(s.g[h].at[0], s.g_recv[h].at[source(k)])

        def step(q, acc):
            arrived(14 - 2 * q)
            arrived(13 - 2 * q)
            return acc + pair([source(14 - 2 * q), source(13 - 2 * q)])

        acc = lax.fori_loop(0, 7, step, jnp.zeros(s.y[h].shape, F32))
        arrived(0)
        return acc + pair([f, source(0)])

    def send_g(h):
        at = s.g[h].at[f]
        loop(0, 15, lambda k: remote(at, at, s.g_send[h], s.g_recv[h].at[f],
                                     dev(z, c, plane(k))).start())

    for h in range(4, 0, -1):
        if h < 4:
            s.w[h][...] = (s.y[h][...] - reaction(h)).astype(BF)
        table = maps[h - 1]
        first = 2 * z if h == 1 else z // 2 ** (h - 2)

        def select(ks, child, h=h, table=table, first=first):
            at = [table[first + child, plane(k)] for k in ks]
            part = dot(s.w[h][...], side_by_side(s.vblk[h][jnp.minimum(a, 32)] for a in at), NN)
            blocks = [part[:, n * 128:(n + 1) * 128] for n in range(4)]
            if here(ks[3]) and h < 4:
                kept = jnp.where(at[3] >= 32, at[3] - 32, 16)
                blocks[3] = blocks[3] + s.g[h][kept].astype(F32)
            return blocks

        def down(ks, h=h, select=select):
            for child in range(2 if h == 1 else 1):
                for k, block in zip(ks, select(ks, child)):
                    s.sel_out[h][plane(k), child * 64:(child + 1) * 64] = block.astype(BF)
            for k in ks:
                i = plane(k)
                if not here(k):
                    remote(s.sel_out[h].at[i], s.sel_in[h].at[k], s.sel_send[h], s.sel_recv[h],
                           dev(z, c, i)).start()

        by_fours(down)

        n, zrel, _ = group(h)
        half = 32 >> h
        for part in range(2):
            def x_step(q, h=h, half=half, zrel=zrel, part=part):
                both = dot(s.w[h][...], columns(s.v[h], zrel * 2 * half + part * half + 2 * q, 2),
                           NN).astype(BF)
                s.x_out[h][part, 2 * q] = both[:, :128]
                s.x_out[h][part, 2 * q + 1] = both[:, 128:]

            loop(0, half // 2, x_step)

        def send_x(k, h=h, n=n):
            remote(s.x_out[h].at[:, plane(k) // n], s.x_in[h].at[k], s.x_send[h],
                   s.x_recv[h], dev(z, c, plane(k))).start()

        loop(0, 15, send_x)
        if h < 4:
            take_x(h + 1)

        wait(s.sel_in[h], s.sel_recv[h])
        total = summed(s.sel_in[h], s.sel_out[h][f].astype(F32)).astype(BF)
        if h > 1:
            s.g[h - 1][f] = total
        else:
            s.g_half[0] = total[:64]
            s.g_half[1] = total[64:]
            half = s.g[0].at[f, rows(c * 64, 64)]
            s.g[0][f, rows(c * 64, 64)] = s.g_half[c]
            remote(s.g_half.at[other], half, s.g_swap.at[0], s.g_swap.at[1],
                   dev(z, other, f)).start()
            wait(half, s.g_swap.at[1])
        send_g(h - 1)
        if h < 4:
            give_x(h + 1)

    w0 = (s.y[0][...] - reaction(0)).astype(BF)

    def x0_block(k):
        return dot(w0, columns(s.v[0], 2 * k, 2), NN)

    def x0_give(k):
        both = x0_block(k).astype(BF)
        s.x0_out[k, 0] = both[:, :128]
        s.x0_out[k, 1] = both[:, 128:]
        remote(s.x0_out.at[k], s.x0_in.at[f], s.x0_send.at[k], s.x0_recv.at[f],
               dev(z, c, k)).start()

    def x0_maybe(k):
        to = plane(k)

        @pl.when(to < f)
        def _():
            x0_give(to)

    loop(0, 15, x0_maybe)
    mine = x0_block(f)
    s.x0_sum[0] = mine[:, :128]
    s.x0_sum[1] = mine[:, 128:]
    take_x(1)

    def x0_take(k):
        wait(s.x0_in.at[k], s.x0_recv.at[k])
        s.x0_sum[...] = s.x0_sum[...] + s.x0_in[k].astype(F32)

    loop(f + 1, FRONT, x0_take)
    for k in range(2):
        out[256 + k * 128:256 + (k + 1) * 128, :] = s.x0_sum[k].T
    give_x(1)

    loop(0, f, lambda k: wait(s.x0_out.at[k], s.x0_send.at[k]))
    loop(f + 1, FRONT, lambda k: wait(s.r.at[pl.ds(0, 2)], s.r_send.at[k]))
    wait(s.up_in[0], s.up_send[0])
    wait(s.g_half.at[0], s.g_swap.at[0])
    wait(s.g[0].at[pl.ds(0, 15)], s.g_send[0])
    for h in range(1, 5):
        n = 2 ** (h - 1)
        m = 256 >> h
        wait(s.v[h].at[pl.ds(0, 128)], s.v_fwd[h].at[0])
        if h < 4:
            wait(s.u[h].at[pl.ds(0, 128)], s.u_fwd[h].at[0])
        if n > 1:
            wait(s.v[h].at[pl.ds(0, (n - 1) * m)], s.v_send[h])
            if h < 4:
                wait(s.u[h].at[pl.ds(0, (n - 1) * m)], s.u_send[h])
            wait(s.zb[h].at[pl.ds(0, (n - 1) * m)], s.zb_send[h])
        away = jnp.int32(0)
        for zr in range(n):
            co, fo, _ = block_owner(h, zr)
            away = away + jnp.where(jnp.logical_and(co == c, fo == f), 0, 1)
        for count in range(max(n - 1, 1), n + 1):
            @pl.when(away == count)
            def _(count=count, h=h, m=m):
                wait(s.bn[h].at[pl.ds(0, count * m)], s.bn_send[h])
        wait(s.b[h].at[pl.ds(0, 30)], s.b_send[h])
        wait(s.b[h].at[0], s.b_swap[h].at[0])
        wait(s.vb[h].at[0, 0], s.swap[h].at[0])
        wait(s.sel_in[h], s.sel_send[h])
        wait(s.vb[h].at[:, pl.ds(0, 15)], s.vb_send[h])
        wait(s.x_in[h], s.x_send[h])
        wait(s.x_sum[h].at[0], s.xx[h].at[0])
        if h < 4:
            wait(s.up_in[h], s.up_send[h])
            wait(s.g[h].at[pl.ds(0, 15)], s.g_send[h])


def hand_out(packed_rows, *refs):
    outs, sems = refs[:5], refs[5]
    copies = [pltpu.make_async_copy(packed_rows.at[pl.ds(256 >> h, 256 >> h)], outs[h].at[0, 0],
                                    sems.at[h]) for h in LEVELS]
    for copy in copies:
        copy.start()
    for copy in copies:
        copy.wait()


def on_device(*args):
    in_hbm = pl.BlockSpec(memory_space=pltpu.HBM)
    smem = pl.BlockSpec(memory_space=pltpu.SMEM)
    vmem = pl.BlockSpec(memory_space=pltpu.VMEM)
    packed_rows = pl.pallas_call(
        kernel,
        out_shape=jax.ShapeDtypeStruct((512, 128), F32),
        in_specs=[in_hbm] * 14 + [smem] * 4,
        out_specs=vmem,
        scratch_shapes=flat(scratch_shapes()),
        compiler_params=pltpu.CompilerParams(
            collective_id=0, has_side_effects=True, vmem_limit_bytes=56 * 2 ** 20),
        name="solve",
    )(*args)
    return tuple(pl.pallas_call(
        hand_out,
        out_shape=[jax.ShapeDtypeStruct(a.shape, F32) for a in args[:5]],
        in_specs=[vmem],
        out_specs=[in_hbm] * 5,
        scratch_shapes=[pltpu.SemaphoreType.DMA((5,))],
        name="hand_out",
    )(packed_rows))


def solution(mesh):
    shard = P("leaf", "front", None, None)
    return jax.shard_map(
        on_device,
        mesh=mesh,
        in_specs=(shard,) * 14 + (P(),) * 4,
        out_specs=(shard,) * 5,
        check_vma=False,
    )
```

```python
import types

import jax
import jax.numpy as jnp
from jax import lax
from jax.experimental import pallas as pl
from jax.experimental.pallas import tpu as pltpu
from jax.sharding import PartitionSpec as P

MESH = pl.DeviceIdType.MESH
BF = jnp.bfloat16
F32 = jnp.float32
NT = (((1,), (1,)), ((), ()))
NN = (((1,), (0,)), ((), ()))
FRONT = 16
LEVELS = range(5)
SHARE = (128, 64, 32, 16, 16)


def packed(numbers):
    return sum(n << 2 * i for i, n in enumerate(numbers))


STEPS = sorted(((dx, dy) for dx in range(4) for dy in range(4)),
               key=lambda s: -min(s[0], 4 - s[0]) - min(s[1], 4 - s[1]))
STEPS_X = packed(s[0] for s in STEPS[:15])
STEPS_Y = packed(s[1] for s in STEPS[:15])


def dot(a, b, dims):
    return lax.dot_general(a, b, dims, preferred_element_type=F32)


def side_by_side(parts):
    return jnp.concatenate(list(parts), axis=1)


def scratch_shapes():
    dma = pltpu.SemaphoreType.DMA

    def vm(*shape, dtype=BF):
        return pltpu.VMEM(shape, dtype)

    def per(make, levels):
        return [make(h) if h in levels else None for h in LEVELS]

    t = types.SimpleNamespace()
    low, high, every, lowered = range(0, 1), range(1, 5), range(0, 5), range(1, 4)
    t.v = per(lambda h: vm(256, 4096), every)
    t.u = per(lambda h: vm(256, 2048), range(0, 4))
    t.vblk = per(lambda h: vm(33, 256, 128), high)
    t.v_load = per(lambda h: dma(()), every)
    t.u_load = per(lambda h: dma(()), range(0, 4))
    t.v_send = per(lambda h: dma(()), range(2, 5))
    t.v_ring = dma((8,))
    t.u_send = per(lambda h: dma(()), range(2, 4))
    t.v_fwd = per(lambda h: dma((2,)), high)
    t.u_fwd = per(lambda h: dma((2,)), lowered)
    t.side = vm(256, 128)
    t.side_load = dma(())
    t.r = vm(32, 128, 128)
    t.r_send = dma((16,))
    t.r_recv = dma((16,))
    t.zb = per(lambda h: vm(128, 128), range(2, 5))
    t.zb_send = per(lambda h: dma(()), range(2, 5))
    t.zb_recv = per(lambda h: dma(()), range(2, 5))
    t.bn = per(lambda h: vm(128, 128), high)
    t.bn_send = per(lambda h: dma(()), high)
    t.bn_recv = per(lambda h: dma(()), high)
    t.bh = per(lambda h: vm(128 // SHARE[h], SHARE[h], 128), high)
    t.b = per(lambda h: vm(32, SHARE[h], 128), high)
    t.b_swap = per(lambda h: dma((2,)), high)
    t.b_send = per(lambda h: dma(()), high)
    t.b_recv = per(lambda h: dma(()), high)
    t.up_out = per(lambda h: vm(16, SHARE[h], 128), range(0, 4))
    t.up_in = per(lambda h: vm(15, SHARE[h], 128), range(0, 4))
    t.up_send = per(lambda h: dma(()), range(0, 4))
    t.up_recv = per(lambda h: dma(()), range(0, 4))
    t.halves = per(lambda h: vm(2, SHARE[h], 128), lowered)
    t.vb = per(lambda h: vm(2, 17, SHARE[h], 128), high)
    t.swap = per(lambda h: dma((2,)), high)
    t.vb_send = per(lambda h: dma(()), high)
    t.vb_recv = per(lambda h: dma((2, 16)), high)
    t.y = per(lambda h: vm(SHARE[h], 256, dtype=F32), range(0, 2))
    t.yz = per(lambda h: vm(64 // SHARE[h], SHARE[h], 256, dtype=F32), range(2, 5))
    t.yz_send = per(lambda h: dma(()), range(2, 5))
    t.yz_recv = per(lambda h: dma(()), range(2, 5))
    t.w = per(lambda h: vm(64, 256), high)
    t.w4 = vm(16, 256)
    t.sel_out = per(lambda h: vm(16, (0, 128, 64, 64, 16)[h], 128), high)
    t.sel_in = per(lambda h: vm(15, (0, 128, 64, 64, 16)[h], 128), high)
    t.gz = dma((2,))
    t.sel_send = per(lambda h: dma(()), high)
    t.sel_recv = per(lambda h: dma(()), high)
    t.g_half = vm(2, 64, 128)
    t.g_swap = dma((2,))
    t.g = per(lambda h: vm(16, 128, 128) if h == 0 else vm(17, 64, 128), range(0, 4))
    t.g_send = per(lambda h: dma(()), range(0, 4))
    t.g_recv = per(lambda h: dma((16,)), range(0, 4))
    t.x_out = per(lambda h: vm(2, 16, 64, 128), high)
    t.x_in = per(lambda h: vm(15, 2, 64, 128), high)
    t.x_send = per(lambda h: dma(()), high)
    t.x_recv = per(lambda h: dma(()), high)
    t.x_sum = per(lambda h: vm(2, 64, 128, dtype=F32), high)
    t.x_full = per(lambda h: vm(2, 64, 128, dtype=F32), high)
    t.x_rows = per(lambda h: vm(128, 128, dtype=F32), high)
    t.xx = per(lambda h: dma((2,)), high)
    t.x0_out = vm(16, 2, 128, 128)
    t.x0_in = vm(16, 2, 128, 128)
    t.x0_sum = vm(2, 128, 128, dtype=F32)
    t.x0_send = dma((16,))
    t.x0_recv = dma((16,))
    return t


def flat(t):
    out = []
    for entry in vars(t).values():
        out += [e for e in entry if e is not None] if isinstance(entry, list) else [entry]
    return out


def unflat(t, refs):
    refs = iter(refs)
    s = types.SimpleNamespace()
    for name, entry in vars(t).items():
        if isinstance(entry, list):
            vars(s)[name] = [None if e is None else next(refs) for e in entry]
        else:
            vars(s)[name] = next(refs)
    return s


def kernel(*refs):
    sides = refs[0:5]
    invs = refs[5:10]
    lows = refs[10:14]
    maps = refs[14:18]
    out = refs[18]
    s = unflat(scratch_shapes(), refs[19:])

    leaf = lax.axis_index("leaf")
    f = lax.axis_index("front")
    z = leaf // 2
    c = leaf % 2
    other = 1 - c

    def dev(z_, c_, f_):
        return (2 * z_ + c_, f_)

    def remote(src, dst, send, recv, device):
        return pltpu.make_async_remote_copy(
            src_ref=src, dst_ref=dst, send_sem=send, recv_sem=recv,
            device_id=device, device_id_type=MESH)

    def wait(ref, sem):
        pltpu.make_async_copy(ref, ref, sem).wait()

    def loop(lo, hi, body):
        lax.fori_loop(lo, hi, lambda i, carry: (body(i), carry)[1], 0)

    fx, fy = f // 4, f % 4

    def step_of(k):
        if isinstance(k, int):
            return STEPS[k]
        return (STEPS_X >> 2 * k) % 4, (STEPS_Y >> 2 * k) % 4

    def plane(k):
        dx, dy = step_of(k)
        return (fx + dx) % 4 * 4 + (fy + dy) % 4

    def source(k):
        dx, dy = step_of(k)
        return (fx + 4 - dx) % 4 * 4 + (fy + 4 - dy) % 4

    def group(h):
        n = 2 ** (h - 1)
        zrel = z % n
        return n, zrel, z - zrel

    def share(h):
        return (0, 0, z % 2, z % 2 * 2 + z // 2 % 2, z % 2 * 2 + z // 2 % 2)[h]

    def own(ref):
        return ref.at[0, 0]

    def rows(first, count):
        return pl.ds(pl.multiple_of(first, count), count)

    def columns(ref, block, count=1):
        return ref[:, pl.ds(pl.multiple_of(block * 128, 128 * count), 128 * count)]

    side_copy = pltpu.make_async_copy(own(sides[0]), s.side, s.side_load)
    side_copy.start()
    barrier = pltpu.get_barrier_semaphore()

    def greet_plane(d):
        q = (c * FRONT + f + d) % (2 * FRONT)
        pl.semaphore_signal(barrier, inc=1, device_id=dev(z, q // FRONT, q % FRONT),
                            device_id_type=MESH)

    def greet_line(d):
        pl.semaphore_signal(barrier, inc=1, device_id=dev((z + d) % 8, c, f),
                            device_id_type=MESH)

    loop(1, 2 * FRONT, greet_plane)
    loop(1, 8, greet_line)
    load_v0 = pltpu.make_async_copy(own(invs[0]), s.v[0], s.v_load[0])
    load_u0 = pltpu.make_async_copy(own(lows[0]), s.u[0], s.u_load[0])
    load_v0.start()
    load_u0.start()
    for h in range(1, 5):
        n, zrel, _ = group(h)
        m = 256 >> h
        at = rows(c * 128 + zrel * m, m)
        pltpu.make_async_copy(own(invs[h]), s.v[h].at[at], s.v_load[h]).start()
        if h < 4:
            pltpu.make_async_copy(own(lows[h]), s.u[h].at[at], s.u_load[h]).start()
        if h > 1:
            pltpu.make_async_copy(own(sides[h]), s.zb[h].at[rows(zrel * m, m)], s.zb_recv[h]).start()
    side_copy.wait()
    for k in range(2):
        s.r[2 * f + k] = s.side[k * 128:(k + 1) * 128, :].astype(F32).T.astype(BF)
    for h in range(1, 5):
        s.vb[h][0, 16] = jnp.zeros((SHARE[h], 128), BF)
        s.vb[h][1, 16] = jnp.zeros((SHARE[h], 128), BF)
        s.vblk[h][32] = jnp.zeros((256, 128), BF)
        if h < 4:
            s.g[h][16] = jnp.zeros((64, 128), BF)
    pl.semaphore_wait(barrier, 31 + 7)

    def send_b0(k):
        to = plane(k)

        @pl.when(to > f)
        def _():
            mine = s.r.at[pl.ds(2 * f, 2)]
            remote(mine, mine, s.r_send.at[to], s.r_recv.at[f], dev(z, c, to)).start()

    loop(0, 15, send_b0)

    def block_owner(h, zr):
        n = 2 ** (h - 1)
        m = 256 >> h
        p = (2 * zr + c) * (32 >> h) + f // n
        return p % 2, p // 2, (f % n) * m

    def send_block_rows(h, src, zr):
        m = 256 >> h
        co, fo, row = block_owner(h, zr)
        dst = s.bn[h].at[rows(row, m)]
        here = jnp.logical_and(co == c, fo == f)

        @pl.when(here)
        def _():
            pltpu.make_async_copy(src, dst, s.bn_recv[h]).start()

        @pl.when(jnp.logical_not(here))
        def _():
            remote(src, dst, s.bn_send[h], s.bn_recv[h], dev(z, co, fo)).start()

    def gather_factor(h, ref, mine, send, load):
        n, zrel, zbase = group(h)
        m = 256 >> h
        dst = ref.at[rows(c * 128 + zrel * m, m)]
        for d in range(1, n):
            remote(own(mine), dst, send, load, dev(zbase + (zrel + d) % n, c, f)).start()

    def gather_level(h):
        gather_factor(h, s.v[h], invs[h], s.v_send[h], s.v_load[h])
        gather_factor(h, s.u[h], lows[h], s.u_send[h], s.u_load[h])

    def forward_factor(ref, load, fwd):
        part = ref.at[rows(c * 128, 128)]
        if load is not None:
            wait(part, load)
        remote(part, part, fwd.at[0], fwd.at[1], dev(z, other, f)).start()

    def ring(step):
        def rows_of(d):
            return s.v[4].at[rows(c * 128 + (z + 8 + d) % 8 * 16, 16)]

        def pass_on(d, to):
            remote(rows_of(d), rows_of(d), s.v_send[4], s.v_ring.at[(z + 8 + d) % 8],
                   dev((z + 8 + to) % 8, c, f)).start()

        def arrived(d):
            wait(rows_of(d), s.v_ring.at[(z + 8 + d) % 8])

        if step == 1:
            wait(rows_of(0), s.v_load[4])
            pass_on(0, 1)
            pass_on(0, -1)
        elif step < 4:
            arrived(1 - step)
            pass_on(1 - step, 1)
            arrived(step - 1)
            pass_on(step - 1, -1)
        elif step == 4:
            arrived(-3)
            pass_on(-3, 1)
        else:
            arrived(3)
            arrived(-4)

    def forward_level(h):
        forward_factor(s.v[h], s.v_load[h] if h < 4 else None, s.v_fwd[h])
        if h < 4:
            forward_factor(s.u[h], s.u_load[h], s.u_fwd[h])

    def have_forward(ref, fwd):
        wait(ref.at[rows(other * 128, 128)], fwd.at[1])

    send_block_rows(1, own(sides[1]), 0)
    for h in range(2, 5):
        n, zrel, zbase = group(h)
        m = 256 >> h
        for d in range(1, n):
            remote(own(sides[h]), s.zb[h].at[rows(zrel * m, m)], s.zb_send[h], s.zb_recv[h],
                   dev(zbase + (zrel + d) % n, c, f)).start()
    gather_level(2)
    gather_level(3)
    forward_level(1)

    load_v0.wait()

    def y0_term(k):
        return dot(side_by_side([s.r[2 * k], s.r[2 * k + 1]]), columns(s.v[0], 2 * k, 2), NT)

    def y0_step(d, acc):
        k = f - d
        wait(s.r.at[pl.ds(0, 2)], s.r_recv.at[k])
        return acc + y0_term(k)

    y0 = lax.fori_loop(1, f + 1, y0_step, y0_term(f))
    s.y[0][...] = y0
    y0 = y0.astype(BF)
    load_u0.wait()

    def by_fours(body):
        loop(0, 3, lambda q: body([4 * q, 4 * q + 1, 4 * q + 2, 4 * q + 3]))
        body([12, 13, 14, 15])

    def here(k):
        return isinstance(k, int) and k == 15

    def up(h, y):
        def four(ks):
            part = dot(y, side_by_side(columns(s.u[h], plane(k)) for k in ks), NN).astype(BF)
            for n, k in enumerate(ks):
                i = plane(k)
                s.up_out[h][i] = part[:, n * 128:(n + 1) * 128]
                if not here(k):
                    remote(s.up_out[h].at[i], s.up_in[h].at[k], s.up_send[h], s.up_recv[h],
                           dev(z, c, i)).start()

        by_fours(four)

    up(0, y0)

    def turn_b(h):
        wait(s.bn[h], s.bn_recv[h])
        turned = s.bn[h][...].astype(F32).T.astype(BF)
        s.bh[h][...] = turned.reshape(s.bh[h].shape)
        block = 2 * f + c
        shares = 64 // SHARE[h]
        s.b[h][block] = s.bh[h][c * shares + share(h)]
        remote(s.bh[h].at[other * shares + share(h)], s.b[h].at[block], s.b_swap[h].at[0],
               s.b_swap[h].at[1], dev(z, other, f)).start()

    def spread_b(h):
        wait(s.b[h].at[0], s.b_swap[h].at[1])
        both = s.b[h].at[pl.ds(2 * f, 2)]
        loop(0, 15, lambda k: remote(both, both, s.b_send[h], s.b_recv[h],
                                     dev(z, c, plane(k))).start())

    def split_columns(h):
        have_forward(s.v[h], s.v_fwd[h])

        def one(k):
            s.vblk[h][k] = columns(s.v[h], k)

        loop(0, 32, one)

    turn_b(1)
    for h in range(2, 5):
        m = 256 >> h
        wait(s.zb[h], s.zb_recv[h])
        for zr in range(2 ** (h - 1)):
            send_block_rows(h, s.zb[h].at[pl.ds(zr * m, m)], zr)
    split_columns(1)
    spread_b(1)

    def send_child(h, child, kind):
        at = s.vb[h].at[child, f]
        loop(0, 15, lambda k: remote(at, at, s.vb_send[h], s.vb_recv[h].at[kind, f],
                                     dev(z, c, plane(k))).start())

    def side_term(h):
        wait(s.b[h].at[pl.ds(0, 30)], s.b_recv[h])

        def step(j, acc):
            part = side_by_side(s.b[h][8 * j + k] for k in range(8))
            return acc + dot(part, columns(s.v[h], 8 * j, 8), NT)

        return lax.fori_loop(0, 4, step, jnp.zeros((SHARE[h], 256), F32))

    def child_term(h, child, kind, acc):
        table = maps[h - 1]
        row = 2 * (z // 2 ** (h - 1)) + child

        def pair(ks):
            at = [jnp.minimum(table[row, k], 32) for k in ks]
            return dot(side_by_side(s.vb[h][child, k] for k in ks),
                       side_by_side(s.vblk[h][a] for a in at), NT)

        def arrived(k):
            wait(s.vb[h].at[0, 0], s.vb_recv[h].at[kind, source(k)])

        def step(q, acc):
            arrived(14 - 2 * q)
            arrived(13 - 2 * q)
            return acc - pair([source(14 - 2 * q), source(13 - 2 * q)])

        acc = lax.fori_loop(0, 7, step, acc)
        arrived(0)
        return acc - pair([f, source(0)])

    def bottom_block(h, child):
        table = maps[h - 1]
        row = 2 * (z // 2 ** (h - 1)) + child
        less = jnp.int32(0)
        hit = jnp.int32(0)
        for i in range(16):
            less = less + (table[row, i] < 32 + f).astype(jnp.int32)
            hit = hit + (table[row, i] == 32 + f).astype(jnp.int32)
        return jnp.where(hit > 0, less, 16)

    def summed(ref, first):
        total = first
        for k in range(15):
            total = total + ref[k].astype(F32)
        return total

    def give_blocks(h, mine, half, sibling):
        remote(half, s.vb[h].at[mine, f], s.swap[h].at[0], s.swap[h].at[1], sibling).start()
        send_child(h, mine, 0)
        wait(s.vb[h].at[mine, f], s.swap[h].at[1])
        send_child(h, 1 - mine, 1)

    wait(s.up_in[0], s.up_recv[0])
    total = summed(s.up_in[0], s.up_out[0][f].astype(F32)).astype(BF)
    s.halves[1][...] = total.reshape(2, 64, 128)
    s.vb[1][c, f] = s.halves[1][c]
    give_blocks(1, c, s.halves[1].at[other], dev(z, other, f))
    for h in range(2, 5):
        turn_b(h)

    for h in range(1, 5):
        mine = c if h == 1 else z // 2 ** (h - 2) % 2
        acc = side_term(h)
        acc = child_term(h, mine, 0, acc)
        acc = child_term(h, 1 - mine, 1, acc)
        y = acc.astype(BF)
        if h == 1:
            s.y[1][...] = acc
        else:
            n = 64 // SHARE[h]
            mine = s.yz[h].at[share(h)]
            s.yz[h][share(h)] = acc
            for d in range(1, n):
                remote(mine, mine, s.yz_send[h], s.yz_recv[h],
                       dev(z - z % n + (z + d) % n, c, f)).start()
        if h == 4:
            s.w4[...] = y
            break
        have_forward(s.u[h], s.u_fwd[h])
        up(h, y)
        spread_b(h + 1)
        if h < 3:
            forward_level(h + 1)
        if h > 1:
            ring(2 * h - 2)
        bottom = [bottom_block(h, child) for child in range(2)]
        if h < 3:
            split_columns(h + 1)
        kept = s.vb[h][0, bottom[0]].astype(F32) + s.vb[h][1, bottom[1]].astype(F32)
        kept = kept + s.up_out[h][f].astype(F32)
        wait(s.up_in[h], s.up_recv[h])
        step = 2 ** (h - 1)
        mine = z // step % 2
        total = summed(s.up_in[h], kept).astype(BF)
        if h < 3:
            s.halves[h + 1][...] = total.reshape(s.halves[h + 1].shape)
            s.vb[h + 1][mine, f] = s.halves[h + 1][mine]
            half = s.halves[h + 1].at[1 - mine]
        else:
            s.vb[4][mine, f] = total
            half = s.vb[4].at[mine, f]
        give_blocks(h + 1, mine, half, dev(z + step - 2 * step * mine, c, f))
        if h < 3:
            ring(2 * h - 1)
        else:
            ring(5)
            forward_level(4)
            split_columns(4)

    def take_x(h):
        wait(s.x_in[h], s.x_recv[h])
        n = 2 ** (h - 1)
        s.x_sum[h][...] = summed(s.x_in[h], s.x_out[h][:, f // n].astype(F32))
        s.x_full[h][c] = s.x_sum[h][c]
        remote(s.x_sum[h].at[other], s.x_full[h].at[c], s.xx[h].at[0], s.xx[h].at[1],
               dev(z, other, f)).start()

    def give_x(h):
        wait(s.x_full[h].at[0], s.xx[h].at[1])
        n = 2 ** (h - 1)
        m = 256 >> h
        s.x_rows[h][...] = s.x_full[h][...].reshape(128, 128).T
        out[m:2 * m, :] = s.x_rows[h][rows((f % n) * m, m), :]

    def reaction(h):
        def pair(ks):
            return dot(side_by_side(s.g[h][k] for k in ks),
                       side_by_side(columns(s.u[h], k) for k in ks), NT)

        def arrived(k):
            wait(s.g[h].at[0], s.g_recv[h].at[source(k)])

        def step(q, acc):
            arrived(14 - 2 * q)
            arrived(13 - 2 * q)
            return acc + pair([source(14 - 2 * q), source(13 - 2 * q)])

        acc = lax.fori_loop(0, 7, step, jnp.zeros((128 if h == 0 else 64, 256), F32))
        arrived(0)
        return acc + pair([f, source(0)])

    def send_rows(h):
        n, zrel, _ = group(h)
        half = 32 >> h
        for part in range(2):
            def x_step(q, part=part):
                both = dot(s.w[h][...], columns(s.v[h], zrel * 2 * half + part * half + 2 * q, 2),
                           NN).astype(BF)
                s.x_out[h][part, 2 * q] = both[:, :128]
                s.x_out[h][part, 2 * q + 1] = both[:, 128:]

            loop(0, half // 2, x_step)

        loop(0, 15, lambda k: remote(s.x_out[h].at[:, plane(k) // n], s.x_in[h].at[k], s.x_send[h],
                                     s.x_recv[h], dev(z, c, plane(k))).start())

    def send_g(h):
        at = s.g[h].at[f]
        loop(0, 15, lambda k: remote(at, at, s.g_send[h], s.g_recv[h].at[f],
                                     dev(z, c, plane(k))).start())

    for h in range(4, 0, -1):
        if h == 1:
            s.w[1][...] = (s.y[1][...] - reaction(1)).astype(BF)
        elif h < 4:
            react = reaction(h)
            wait(s.yz[h].at[pl.ds(1, 64 // SHARE[h] - 1)], s.yz_recv[h])
            s.w[h][...] = (s.yz[h][...].reshape(64, 256) - react).astype(BF)
        w_sel = s.w4 if h == 4 else s.w[h]
        table = maps[h - 1]
        first = 2 * z if h == 1 else z // 2 ** (h - 2)

        def select(ks, child, h=h, table=table, first=first, w_sel=w_sel):
            at = [table[first + child, plane(k)] for k in ks]
            part = dot(w_sel[...], side_by_side(s.vblk[h][jnp.minimum(a, 32)] for a in at), NN)
            blocks = [part[:, n * 128:(n + 1) * 128] for n in range(4)]
            if here(ks[3]) and h < 4:
                kept = jnp.where(at[3] >= 32, at[3] - 32, 16)
                blocks[3] = blocks[3] + s.g[h][kept].astype(F32)
            return blocks

        def down(ks, h=h, select=select):
            for child in range(2 if h == 1 else 1):
                for k, block in zip(ks, select(ks, child)):
                    n = block.shape[0]
                    s.sel_out[h][plane(k), child * n:(child + 1) * n] = block.astype(BF)
            for k in ks:
                i = plane(k)
                if not here(k):
                    remote(s.sel_out[h].at[i], s.sel_in[h].at[k], s.sel_send[h], s.sel_recv[h],
                           dev(z, c, i)).start()

        by_fours(down)

        if h < 4:
            send_rows(h)
        if h < 4:
            take_x(h + 1)

        wait(s.sel_in[h], s.sel_recv[h])
        total = summed(s.sel_in[h], s.sel_out[h][f].astype(F32)).astype(BF)
        if h == 4:
            mine = s.g[3].at[f, rows(share(4) * 16, 16)]
            s.g[3][f, rows(share(4) * 16, 16)] = total
            for d in range(1, 4):
                remote(mine, mine, s.gz.at[0], s.gz.at[1], dev(z - z % 4 + (z + d) % 4, c, f)).start()
            wait(s.g[3].at[f, pl.ds(0, 48)], s.gz.at[1])
        elif h > 1:
            s.g[h - 1][f] = total
        else:
            s.g_half[0] = total[:64]
            s.g_half[1] = total[64:]
            half = s.g[0].at[f, rows(c * 64, 64)]
            s.g[0][f, rows(c * 64, 64)] = s.g_half[c]
            remote(s.g_half.at[other], half, s.g_swap.at[0], s.g_swap.at[1],
                   dev(z, other, f)).start()
            wait(half, s.g_swap.at[1])
        send_g(h - 1)
        if h < 4:
            give_x(h + 1)
        else:
            wait(s.yz[4].at[pl.ds(1, 3)], s.yz_recv[4])
            s.w[4][...] = s.yz[4][...].reshape(64, 256).astype(BF)
            send_rows(4)

    w0 = (s.y[0][...] - reaction(0)).astype(BF)

    def x0_block(k):
        return dot(w0, columns(s.v[0], 2 * k, 2), NN)

    def x0_give(k):
        both = x0_block(k).astype(BF)
        s.x0_out[k, 0] = both[:, :128]
        s.x0_out[k, 1] = both[:, 128:]
        remote(s.x0_out.at[k], s.x0_in.at[f], s.x0_send.at[k], s.x0_recv.at[f],
               dev(z, c, k)).start()

    def x0_maybe(k):
        to = plane(k)

        @pl.when(to < f)
        def _():
            x0_give(to)

    loop(0, 15, x0_maybe)
    mine = x0_block(f)
    s.x0_sum[0] = mine[:, :128]
    s.x0_sum[1] = mine[:, 128:]
    take_x(1)

    def x0_take(k):
        wait(s.x0_in.at[k], s.x0_recv.at[k])
        s.x0_sum[...] = s.x0_sum[...] + s.x0_in[k].astype(F32)

    loop(f + 1, FRONT, x0_take)
    for k in range(2):
        out[256 + k * 128:256 + (k + 1) * 128, :] = s.x0_sum[k].T
    give_x(1)

    loop(0, f, lambda k: wait(s.x0_out.at[k], s.x0_send.at[k]))
    loop(f + 1, FRONT, lambda k: wait(s.r.at[pl.ds(0, 2)], s.r_send.at[k]))
    wait(s.up_in[0], s.up_send[0])
    wait(s.g_half.at[0], s.g_swap.at[0])
    wait(s.g[3].at[f, pl.ds(0, 48)], s.gz.at[0])
    wait(s.g[0].at[pl.ds(0, 15)], s.g_send[0])
    for h in range(1, 5):
        n = 2 ** (h - 1)
        m = 256 >> h
        wait(s.v[h].at[pl.ds(0, 128)], s.v_fwd[h].at[0])
        if h < 4:
            wait(s.u[h].at[pl.ds(0, 128)], s.u_fwd[h].at[0])
        if n > 1:
            wait(s.v[h].at[pl.ds(0, (n - 1) * m)], s.v_send[h])
            if h < 4:
                wait(s.u[h].at[pl.ds(0, (n - 1) * m)], s.u_send[h])
            wait(s.zb[h].at[pl.ds(0, (n - 1) * m)], s.zb_send[h])
        away = jnp.int32(0)
        for zr in range(n):
            co, fo, _ = block_owner(h, zr)
            away = away + jnp.where(jnp.logical_and(co == c, fo == f), 0, 1)
        for count in range(max(n - 1, 1), n + 1):
            @pl.when(away == count)
            def _(count=count, h=h, m=m):
                wait(s.bn[h].at[pl.ds(0, count * m)], s.bn_send[h])
        wait(s.b[h].at[pl.ds(0, 30)], s.b_send[h])
        wait(s.b[h].at[0], s.b_swap[h].at[0])
        wait(s.vb[h].at[0, 0], s.swap[h].at[0])
        wait(s.sel_in[h], s.sel_send[h])
        if h > 1:
            wait(s.yz[h].at[pl.ds(1, 64 // SHARE[h] - 1)], s.yz_send[h])
        wait(s.vb[h].at[:, pl.ds(0, 15)], s.vb_send[h])
        wait(s.x_in[h], s.x_send[h])
        wait(s.x_sum[h].at[0], s.xx[h].at[0])
        if h < 4:
            wait(s.up_in[h], s.up_send[h])
            wait(s.g[h].at[pl.ds(0, 15)], s.g_send[h])


def hand_out(packed_rows, *refs):
    outs, sems = refs[:5], refs[5]
    copies = [pltpu.make_async_copy(packed_rows.at[pl.ds(256 >> h, 256 >> h)], outs[h].at[0, 0],
                                    sems.at[h]) for h in LEVELS]
    for copy in copies:
        copy.start()
    for copy in copies:
        copy.wait()


def on_device(*args):
    in_hbm = pl.BlockSpec(memory_space=pltpu.HBM)
    smem = pl.BlockSpec(memory_space=pltpu.SMEM)
    vmem = pl.BlockSpec(memory_space=pltpu.VMEM)
    packed_rows = pl.pallas_call(
        kernel,
        out_shape=jax.ShapeDtypeStruct((512, 128), F32),
        in_specs=[in_hbm] * 14 + [smem] * 4,
        out_specs=vmem,
        scratch_shapes=flat(scratch_shapes()),
        compiler_params=pltpu.CompilerParams(
            collective_id=0, has_side_effects=True, vmem_limit_bytes=56 * 2 ** 20),
        name="solve",
    )(*args)
    return tuple(pl.pallas_call(
        hand_out,
        out_shape=[jax.ShapeDtypeStruct(a.shape, F32) for a in args[:5]],
        in_specs=[vmem],
        out_specs=[in_hbm] * 5,
        scratch_shapes=[pltpu.SemaphoreType.DMA((5,))],
        name="hand_out",
    )(packed_rows))


def solution(mesh):
    shard = P("leaf", "front", None, None)
    return jax.shard_map(
        on_device,
        mesh=mesh,
        in_specs=(shard,) * 14 + (P(),) * 4,
        out_specs=(shard,) * 5,
        check_vma=False,
    )
```

```python
import types

import jax
import jax.numpy as jnp
from jax import lax
from jax.experimental import pallas as pl
from jax.experimental.pallas import tpu as pltpu
from jax.sharding import PartitionSpec as P

MESH = pl.DeviceIdType.MESH
BF = jnp.bfloat16
F32 = jnp.float32
NT = (((1,), (1,)), ((), ()))
NN = (((1,), (0,)), ((), ()))
FRONT = 16
LEVELS = range(5)
SHARE = (128, 64, 32, 16, 16)


def packed(numbers):
    return sum(n << 2 * i for i, n in enumerate(numbers))


STEPS = sorted(((dx, dy) for dx in range(4) for dy in range(4)),
               key=lambda s: -min(s[0], 4 - s[0]) - min(s[1], 4 - s[1]))
STEPS_X = packed(s[0] for s in STEPS[:15])
STEPS_Y = packed(s[1] for s in STEPS[:15])


def dot(a, b, dims):
    return lax.dot_general(a, b, dims, preferred_element_type=F32)


def side_by_side(parts):
    return jnp.concatenate(list(parts), axis=1)


def scratch_shapes():
    dma = pltpu.SemaphoreType.DMA

    def vm(*shape, dtype=BF):
        return pltpu.VMEM(shape, dtype)

    def per(make, levels):
        return [make(h) if h in levels else None for h in LEVELS]

    t = types.SimpleNamespace()
    low, high, every, lowered = range(0, 1), range(1, 5), range(0, 5), range(1, 4)
    t.v = per(lambda h: vm(256, 4096), every)
    t.u = per(lambda h: vm(256, 2048), range(0, 4))
    t.vblk = per(lambda h: vm(33, 256, 128), high)
    t.v_load = per(lambda h: dma(()), every)
    t.u_load = per(lambda h: dma(()), range(0, 4))
    t.v_send = per(lambda h: dma(()), range(2, 5))
    t.v_ring = dma((8,))
    t.u_send = per(lambda h: dma(()), range(2, 4))
    t.v_fwd = per(lambda h: dma((2,)), high)
    t.u_fwd = per(lambda h: dma((2,)), lowered)
    t.side = vm(256, 128)
    t.side_load = dma(())
    t.r = vm(32, 128, 128)
    t.r_send = dma((16,))
    t.r_recv = dma((16,))
    t.zb = per(lambda h: vm(128, 128), range(2, 5))
    t.zb_send = per(lambda h: dma(()), range(2, 5))
    t.zb_recv = per(lambda h: dma(()), range(2, 5))
    t.bn = per(lambda h: vm(128, 128), high)
    t.bn_send = per(lambda h: dma(()), high)
    t.bn_recv = per(lambda h: dma(()), high)
    t.bh = per(lambda h: vm(128 // SHARE[h], SHARE[h], 128), high)
    t.b = per(lambda h: vm(32, SHARE[h], 128), high)
    t.b_swap = per(lambda h: dma((2,)), high)
    t.b_send = per(lambda h: dma(()), high)
    t.b_recv = per(lambda h: dma(()), high)
    t.up_out = per(lambda h: vm(16, SHARE[h], 128), range(0, 4))
    t.up_in = per(lambda h: vm(15, SHARE[h], 128), range(0, 4))
    t.up_send = per(lambda h: dma(()), range(0, 4))
    t.up_recv = per(lambda h: dma(()), range(0, 4))
    t.halves = per(lambda h: vm(2, SHARE[h], 128), lowered)
    t.vb = per(lambda h: vm(2, 17, SHARE[h], 128), high)
    t.swap = per(lambda h: dma((2,)), high)
    t.vb_send = per(lambda h: dma(()), high)
    t.vb_recv = per(lambda h: dma((2, 16)), high)
    t.y = per(lambda h: vm(SHARE[h], 256, dtype=F32), range(0, 2))
    t.yz = per(lambda h: vm(64 // SHARE[h], SHARE[h], 256, dtype=F32), range(2, 5))
    t.yz_send = per(lambda h: dma(()), range(2, 5))
    t.yz_recv = per(lambda h: dma(()), range(2, 5))
    t.w = per(lambda h: vm(64, 256), high)
    t.w4 = vm(16, 256)
    t.sel_out = per(lambda h: vm(16, (0, 128, 64, 64, 16)[h], 128), high)
    t.sel_in = per(lambda h: vm(15, (0, 128, 64, 64, 16)[h], 128), high)
    t.gz = dma((2,))
    t.sel_send = per(lambda h: dma(()), high)
    t.sel_recv = per(lambda h: dma(()), high)
    t.g_half = vm(2, 64, 128)
    t.g_swap = dma((2,))
    t.g = per(lambda h: vm(16, 128, 128) if h == 0 else vm(17, 64, 128), range(0, 4))
    t.g_send = per(lambda h: dma(()), range(0, 4))
    t.g_recv = per(lambda h: dma((16,)), range(0, 4))
    t.x_out = per(lambda h: vm(2, 16, 64, 128) if h == 1 else vm(16, 256 >> h, 128), high)
    t.x_in = per(lambda h: vm(15, 2, 64, 128) if h == 1 else vm(15, 256 >> h, 128), high)
    t.x_send = per(lambda h: dma(()), high)
    t.x_recv = per(lambda h: dma(()), high)
    t.x_sum = per(lambda h: vm(2, 64, 128, dtype=F32) if h == 1 else vm(256 >> h, 128, dtype=F32), high)
    t.x_full = per(lambda h: vm(2, 64, 128, dtype=F32) if h == 1 else vm(256 >> h, 128, dtype=F32), high)
    t.xx = per(lambda h: dma((2,)), high)
    t.x0_out = vm(16, 2, 128, 128)
    t.x0_in = vm(16, 2, 128, 128)
    t.x0_sum = vm(2, 128, 128, dtype=F32)
    t.x0_send = dma((16,))
    t.x0_recv = dma((16,))
    return t


def flat(t):
    out = []
    for entry in vars(t).values():
        out += [e for e in entry if e is not None] if isinstance(entry, list) else [entry]
    return out


def unflat(t, refs):
    refs = iter(refs)
    s = types.SimpleNamespace()
    for name, entry in vars(t).items():
        if isinstance(entry, list):
            vars(s)[name] = [None if e is None else next(refs) for e in entry]
        else:
            vars(s)[name] = next(refs)
    return s


def kernel(*refs):
    sides = refs[0:5]
    invs = refs[5:10]
    lows = refs[10:14]
    maps = refs[14:18]
    out = refs[18]
    s = unflat(scratch_shapes(), refs[19:])

    leaf = lax.axis_index("leaf")
    f = lax.axis_index("front")
    z = leaf // 2
    c = leaf % 2
    other = 1 - c

    def dev(z_, c_, f_):
        return (2 * z_ + c_, f_)

    def remote(src, dst, send, recv, device):
        return pltpu.make_async_remote_copy(
            src_ref=src, dst_ref=dst, send_sem=send, recv_sem=recv,
            device_id=device, device_id_type=MESH)

    def wait(ref, sem):
        pltpu.make_async_copy(ref, ref, sem).wait()

    def loop(lo, hi, body):
        lax.fori_loop(lo, hi, lambda i, carry: (body(i), carry)[1], 0)

    fx, fy = f // 4, f % 4

    def step_of(k):
        if isinstance(k, int):
            return STEPS[k]
        return (STEPS_X >> 2 * k) % 4, (STEPS_Y >> 2 * k) % 4

    def plane(k):
        dx, dy = step_of(k)
        return (fx + dx) % 4 * 4 + (fy + dy) % 4

    def source(k):
        dx, dy = step_of(k)
        return (fx + 4 - dx) % 4 * 4 + (fy + 4 - dy) % 4

    def group(h):
        n = 2 ** (h - 1)
        zrel = z % n
        return n, zrel, z - zrel

    def share(h):
        return (0, 0, z % 2, z % 2 * 2 + z // 2 % 2, z % 2 * 2 + z // 2 % 2)[h]

    def own(ref):
        return ref.at[0, 0]

    def rows(first, count):
        return pl.ds(pl.multiple_of(first, count), count)

    def columns(ref, block, count=1):
        return ref[:, pl.ds(pl.multiple_of(block * 128, 128 * count), 128 * count)]

    side_copy = pltpu.make_async_copy(own(sides[0]), s.side, s.side_load)
    side_copy.start()
    barrier = pltpu.get_barrier_semaphore()

    def greet_plane(d):
        q = (c * FRONT + f + d) % (2 * FRONT)
        pl.semaphore_signal(barrier, inc=1, device_id=dev(z, q // FRONT, q % FRONT),
                            device_id_type=MESH)

    def greet_line(d):
        pl.semaphore_signal(barrier, inc=1, device_id=dev((z + d) % 8, c, f),
                            device_id_type=MESH)

    loop(1, 2 * FRONT, greet_plane)
    loop(1, 8, greet_line)
    load_v0 = pltpu.make_async_copy(own(invs[0]), s.v[0], s.v_load[0])
    load_u0 = pltpu.make_async_copy(own(lows[0]), s.u[0], s.u_load[0])
    load_v0.start()
    load_u0.start()
    for h in range(1, 5):
        n, zrel, _ = group(h)
        m = 256 >> h
        at = rows(c * 128 + zrel * m, m)
        pltpu.make_async_copy(own(invs[h]), s.v[h].at[at], s.v_load[h]).start()
        if h < 4:
            pltpu.make_async_copy(own(lows[h]), s.u[h].at[at], s.u_load[h]).start()
        if h > 1:
            pltpu.make_async_copy(own(sides[h]), s.zb[h].at[rows(zrel * m, m)], s.zb_recv[h]).start()
    side_copy.wait()
    for k in range(2):
        s.r[2 * f + k] = s.side[k * 128:(k + 1) * 128, :].astype(F32).T.astype(BF)
    for h in range(1, 5):
        s.vb[h][0, 16] = jnp.zeros((SHARE[h], 128), BF)
        s.vb[h][1, 16] = jnp.zeros((SHARE[h], 128), BF)
        s.vblk[h][32] = jnp.zeros((256, 128), BF)
        if h < 4:
            s.g[h][16] = jnp.zeros((64, 128), BF)
    pl.semaphore_wait(barrier, 31 + 7)

    def send_b0(k):
        to = plane(k)

        @pl.when(to > f)
        def _():
            mine = s.r.at[pl.ds(2 * f, 2)]
            remote(mine, mine, s.r_send.at[to], s.r_recv.at[f], dev(z, c, to)).start()

    loop(0, 15, send_b0)

    def block_owner(h, zr):
        n = 2 ** (h - 1)
        m = 256 >> h
        p = (2 * zr + c) * (32 >> h) + f // n
        return p % 2, p // 2, (f % n) * m

    def send_block_rows(h, src, zr):
        m = 256 >> h
        co, fo, row = block_owner(h, zr)
        dst = s.bn[h].at[rows(row, m)]
        here = jnp.logical_and(co == c, fo == f)

        @pl.when(here)
        def _():
            pltpu.make_async_copy(src, dst, s.bn_recv[h]).start()

        @pl.when(jnp.logical_not(here))
        def _():
            remote(src, dst, s.bn_send[h], s.bn_recv[h], dev(z, co, fo)).start()

    def gather_factor(h, ref, mine, send, load):
        n, zrel, zbase = group(h)
        m = 256 >> h
        dst = ref.at[rows(c * 128 + zrel * m, m)]
        for d in range(1, n):
            remote(own(mine), dst, send, load, dev(zbase + (zrel + d) % n, c, f)).start()

    def gather_level(h):
        gather_factor(h, s.v[h], invs[h], s.v_send[h], s.v_load[h])
        gather_factor(h, s.u[h], lows[h], s.u_send[h], s.u_load[h])

    def forward_factor(ref, load, fwd):
        part = ref.at[rows(c * 128, 128)]
        if load is not None:
            wait(part, load)
        remote(part, part, fwd.at[0], fwd.at[1], dev(z, other, f)).start()

    def ring(step):
        def rows_of(d):
            return s.v[4].at[rows(c * 128 + (z + 8 + d) % 8 * 16, 16)]

        def pass_on(d, to):
            remote(rows_of(d), rows_of(d), s.v_send[4], s.v_ring.at[(z + 8 + d) % 8],
                   dev((z + 8 + to) % 8, c, f)).start()

        def arrived(d):
            wait(rows_of(d), s.v_ring.at[(z + 8 + d) % 8])

        if step == 1:
            wait(rows_of(0), s.v_load[4])
            pass_on(0, 1)
            pass_on(0, -1)
        elif step < 4:
            arrived(1 - step)
            pass_on(1 - step, 1)
            arrived(step - 1)
            pass_on(step - 1, -1)
        elif step == 4:
            arrived(-3)
            pass_on(-3, 1)
        else:
            arrived(3)
            arrived(-4)

    def forward_level(h):
        forward_factor(s.v[h], s.v_load[h] if h < 4 else None, s.v_fwd[h])
        if h < 4:
            forward_factor(s.u[h], s.u_load[h], s.u_fwd[h])

    def have_forward(ref, fwd):
        wait(ref.at[rows(other * 128, 128)], fwd.at[1])

    send_block_rows(1, own(sides[1]), 0)
    for h in range(2, 5):
        n, zrel, zbase = group(h)
        m = 256 >> h
        for d in range(1, n):
            remote(own(sides[h]), s.zb[h].at[rows(zrel * m, m)], s.zb_send[h], s.zb_recv[h],
                   dev(zbase + (zrel + d) % n, c, f)).start()
    gather_level(2)
    gather_level(3)
    forward_level(1)

    load_v0.wait()

    def y0_term(k):
        return dot(side_by_side([s.r[2 * k], s.r[2 * k + 1]]), columns(s.v[0], 2 * k, 2), NT)

    def y0_step(d, acc):
        k = f - d
        wait(s.r.at[pl.ds(0, 2)], s.r_recv.at[k])
        return acc + y0_term(k)

    y0 = lax.fori_loop(1, f + 1, y0_step, y0_term(f))
    s.y[0][...] = y0
    y0 = y0.astype(BF)
    load_u0.wait()

    def by_fours(body):
        loop(0, 3, lambda q: body([4 * q, 4 * q + 1, 4 * q + 2, 4 * q + 3]))
        body([12, 13, 14, 15])

    def here(k):
        return isinstance(k, int) and k == 15

    def up(h, y):
        def four(ks):
            part = dot(y, side_by_side(columns(s.u[h], plane(k)) for k in ks), NN).astype(BF)
            for n, k in enumerate(ks):
                i = plane(k)
                s.up_out[h][i] = part[:, n * 128:(n + 1) * 128]
                if not here(k):
                    remote(s.up_out[h].at[i], s.up_in[h].at[k], s.up_send[h], s.up_recv[h],
                           dev(z, c, i)).start()

        by_fours(four)

    up(0, y0)

    def turn_b(h):
        wait(s.bn[h], s.bn_recv[h])
        turned = s.bn[h][...].astype(F32).T.astype(BF)
        s.bh[h][...] = turned.reshape(s.bh[h].shape)
        block = 2 * f + c
        shares = 64 // SHARE[h]
        s.b[h][block] = s.bh[h][c * shares + share(h)]
        remote(s.bh[h].at[other * shares + share(h)], s.b[h].at[block], s.b_swap[h].at[0],
               s.b_swap[h].at[1], dev(z, other, f)).start()

    def spread_b(h):
        wait(s.b[h].at[0], s.b_swap[h].at[1])
        both = s.b[h].at[pl.ds(2 * f, 2)]
        loop(0, 15, lambda k: remote(both, both, s.b_send[h], s.b_recv[h],
                                     dev(z, c, plane(k))).start())

    def split_columns(h):
        have_forward(s.v[h], s.v_fwd[h])

        def one(k):
            s.vblk[h][k] = columns(s.v[h], k)

        loop(0, 32, one)

    turn_b(1)
    for h in range(2, 5):
        m = 256 >> h
        wait(s.zb[h], s.zb_recv[h])
        for zr in range(2 ** (h - 1)):
            send_block_rows(h, s.zb[h].at[pl.ds(zr * m, m)], zr)
    split_columns(1)
    spread_b(1)

    def send_child(h, child, kind):
        at = s.vb[h].at[child, f]
        loop(0, 15, lambda k: remote(at, at, s.vb_send[h], s.vb_recv[h].at[kind, f],
                                     dev(z, c, plane(k))).start())

    def side_term(h):
        wait(s.b[h].at[pl.ds(0, 30)], s.b_recv[h])

        def step(j, acc):
            part = side_by_side(s.b[h][8 * j + k] for k in range(8))
            return acc + dot(part, columns(s.v[h], 8 * j, 8), NT)

        return lax.fori_loop(0, 4, step, jnp.zeros((SHARE[h], 256), F32))

    def child_term(h, child, kind, acc):
        table = maps[h - 1]
        row = 2 * (z // 2 ** (h - 1)) + child

        def pair(ks):
            at = [jnp.minimum(table[row, k], 32) for k in ks]
            return dot(side_by_side(s.vb[h][child, k] for k in ks),
                       side_by_side(s.vblk[h][a] for a in at), NT)

        def arrived(k):
            wait(s.vb[h].at[0, 0], s.vb_recv[h].at[kind, source(k)])

        def step(q, acc):
            arrived(14 - 2 * q)
            arrived(13 - 2 * q)
            return acc - pair([source(14 - 2 * q), source(13 - 2 * q)])

        acc = lax.fori_loop(0, 7, step, acc)
        arrived(0)
        return acc - pair([f, source(0)])

    def bottom_block(h, child):
        table = maps[h - 1]
        row = 2 * (z // 2 ** (h - 1)) + child
        less = jnp.int32(0)
        hit = jnp.int32(0)
        for i in range(16):
            less = less + (table[row, i] < 32 + f).astype(jnp.int32)
            hit = hit + (table[row, i] == 32 + f).astype(jnp.int32)
        return jnp.where(hit > 0, less, 16)

    def summed(ref, first):
        total = first
        for k in range(15):
            total = total + ref[k].astype(F32)
        return total

    def give_blocks(h, mine, half, sibling):
        remote(half, s.vb[h].at[mine, f], s.swap[h].at[0], s.swap[h].at[1], sibling).start()
        send_child(h, mine, 0)
        wait(s.vb[h].at[mine, f], s.swap[h].at[1])
        send_child(h, 1 - mine, 1)

    wait(s.up_in[0], s.up_recv[0])
    total = summed(s.up_in[0], s.up_out[0][f].astype(F32)).astype(BF)
    s.halves[1][...] = total.reshape(2, 64, 128)
    s.vb[1][c, f] = s.halves[1][c]
    give_blocks(1, c, s.halves[1].at[other], dev(z, other, f))
    for h in range(2, 5):
        turn_b(h)

    for h in range(1, 5):
        mine = c if h == 1 else z // 2 ** (h - 2) % 2
        acc = side_term(h)
        acc = child_term(h, mine, 0, acc)
        acc = child_term(h, 1 - mine, 1, acc)
        y = acc.astype(BF)
        if h == 1:
            s.y[1][...] = acc
        else:
            n = 64 // SHARE[h]
            mine = s.yz[h].at[share(h)]
            s.yz[h][share(h)] = acc
            for d in range(1, n):
                remote(mine, mine, s.yz_send[h], s.yz_recv[h],
                       dev(z - z % n + (z + d) % n, c, f)).start()
        if h == 4:
            s.w4[...] = y
            break
        have_forward(s.u[h], s.u_fwd[h])
        up(h, y)
        spread_b(h + 1)
        if h < 3:
            forward_level(h + 1)
        if h > 1:
            ring(2 * h - 2)
        bottom = [bottom_block(h, child) for child in range(2)]
        if h < 3:
            split_columns(h + 1)
        kept = s.vb[h][0, bottom[0]].astype(F32) + s.vb[h][1, bottom[1]].astype(F32)
        kept = kept + s.up_out[h][f].astype(F32)
        wait(s.up_in[h], s.up_recv[h])
        step = 2 ** (h - 1)
        mine = z // step % 2
        total = summed(s.up_in[h], kept).astype(BF)
        if h < 3:
            s.halves[h + 1][...] = total.reshape(s.halves[h + 1].shape)
            s.vb[h + 1][mine, f] = s.halves[h + 1][mine]
            half = s.halves[h + 1].at[1 - mine]
        else:
            s.vb[4][mine, f] = total
            half = s.vb[4].at[mine, f]
        give_blocks(h + 1, mine, half, dev(z + step - 2 * step * mine, c, f))
        if h < 3:
            ring(2 * h - 1)
        else:
            ring(5)
            forward_level(4)
            split_columns(4)

    def take_x(h):
        wait(s.x_in[h], s.x_recv[h])
        if h == 1:
            s.x_sum[1][...] = summed(s.x_in[1], s.x_out[1][:, f].astype(F32))
            s.x_full[1][c] = s.x_sum[1][c]
            src, dst = s.x_sum[1].at[other], s.x_full[1].at[c]
        else:
            s.x_sum[h][...] = summed(s.x_in[h], s.x_out[h][f].astype(F32))
            src, dst = s.x_sum[h], s.x_full[h]
        remote(src, dst, s.xx[h].at[0], s.xx[h].at[1], dev(z, other, f)).start()

    def give_x(h):
        m = 256 >> h
        if h == 1:
            wait(s.x_full[1].at[0], s.xx[1].at[1])
            out[m:2 * m, :] = s.x_full[1][...].reshape(128, 128).T
        else:
            wait(s.x_full[h], s.xx[h].at[1])
            theirs = s.x_full[h][...]
            theirs = side_by_side([theirs[:, 64:], theirs[:, :64]])
            lane = lax.broadcasted_iota(jnp.int32, (m, 128), 1)
            out[m:2 * m, :] = jnp.where(lane // 64 == c, s.x_sum[h][...], theirs)

    def reaction(h):
        def pair(ks):
            return dot(side_by_side(s.g[h][k] for k in ks),
                       side_by_side(columns(s.u[h], k) for k in ks), NT)

        def arrived(k):
            wait(s.g[h].at[0], s.g_recv[h].at[source(k)])

        def step(q, acc):
            arrived(14 - 2 * q)
            arrived(13 - 2 * q)
            return acc + pair([source(14 - 2 * q), source(13 - 2 * q)])

        acc = lax.fori_loop(0, 7, step, jnp.zeros((128 if h == 0 else 64, 256), F32))
        arrived(0)
        return acc + pair([f, source(0)])

    def send_rows(h):
        _, zrel, _ = group(h)
        half = 32 >> h
        first = zrel * 2 * half
        w = s.w[h][...]
        if h == 1:
            for part in range(2):
                def x_step(q, part=part):
                    both = dot(w, columns(s.v[1], first + part * half + 2 * q, 2), NN).astype(BF)
                    s.x_out[1][part, 2 * q] = both[:, :128]
                    s.x_out[1][part, 2 * q + 1] = both[:, 128:]

                loop(0, half // 2, x_step)
        else:
            m = 256 >> h

            def row_step(q):
                both = [dot(w, columns(s.v[h], first + part * half + q), NN) for part in range(2)]
                turned = jnp.concatenate(both, axis=0).T.astype(BF)
                s.x_out[h][pl.ds(q * (128 // m), 128 // m)] = turned.reshape(128 // m, m, 128)

            loop(0, half, row_step)

        def send(k):
            src = s.x_out[1].at[:, plane(k)] if h == 1 else s.x_out[h].at[plane(k)]
            remote(src, s.x_in[h].at[k], s.x_send[h], s.x_recv[h], dev(z, c, plane(k))).start()

        loop(0, 15, send)

    def send_g(h):
        at = s.g[h].at[f]
        loop(0, 15, lambda k: remote(at, at, s.g_send[h], s.g_recv[h].at[f],
                                     dev(z, c, plane(k))).start())

    for h in range(4, 0, -1):
        if h == 1:
            s.w[1][...] = (s.y[1][...] - reaction(1)).astype(BF)
        elif h < 4:
            react = reaction(h)
            wait(s.yz[h].at[pl.ds(1, 64 // SHARE[h] - 1)], s.yz_recv[h])
            s.w[h][...] = (s.yz[h][...].reshape(64, 256) - react).astype(BF)
        w_sel = s.w4 if h == 4 else s.w[h]
        table = maps[h - 1]
        first = 2 * z if h == 1 else z // 2 ** (h - 2)

        def select(ks, child, h=h, table=table, first=first, w_sel=w_sel):
            at = [table[first + child, plane(k)] for k in ks]
            part = dot(w_sel[...], side_by_side(s.vblk[h][jnp.minimum(a, 32)] for a in at), NN)
            blocks = [part[:, n * 128:(n + 1) * 128] for n in range(4)]
            if here(ks[3]) and h < 4:
                kept = jnp.where(at[3] >= 32, at[3] - 32, 16)
                blocks[3] = blocks[3] + s.g[h][kept].astype(F32)
            return blocks

        def down(ks, h=h, select=select):
            for child in range(2 if h == 1 else 1):
                for k, block in zip(ks, select(ks, child)):
                    n = block.shape[0]
                    s.sel_out[h][plane(k), child * n:(child + 1) * n] = block.astype(BF)
            for k in ks:
                i = plane(k)
                if not here(k):
                    remote(s.sel_out[h].at[i], s.sel_in[h].at[k], s.sel_send[h], s.sel_recv[h],
                           dev(z, c, i)).start()

        by_fours(down)

        if h < 4:
            take_x(h + 1)

        wait(s.sel_in[h], s.sel_recv[h])
        total = summed(s.sel_in[h], s.sel_out[h][f].astype(F32)).astype(BF)
        if h == 4:
            mine = s.g[3].at[f, rows(share(4) * 16, 16)]
            s.g[3][f, rows(share(4) * 16, 16)] = total
            for d in range(1, 4):
                remote(mine, mine, s.gz.at[0], s.gz.at[1], dev(z - z % 4 + (z + d) % 4, c, f)).start()
            wait(s.g[3].at[f, pl.ds(0, 48)], s.gz.at[1])
        elif h > 1:
            s.g[h - 1][f] = total
        else:
            s.g_half[0] = total[:64]
            s.g_half[1] = total[64:]
            half = s.g[0].at[f, rows(c * 64, 64)]
            s.g[0][f, rows(c * 64, 64)] = s.g_half[c]
            remote(s.g_half.at[other], half, s.g_swap.at[0], s.g_swap.at[1],
                   dev(z, other, f)).start()
            wait(half, s.g_swap.at[1])
        send_g(h - 1)
        if h < 4:
            send_rows(h)
            give_x(h + 1)
        else:
            wait(s.yz[4].at[pl.ds(1, 3)], s.yz_recv[4])
            s.w[4][...] = s.yz[4][...].reshape(64, 256).astype(BF)
            send_rows(4)

    w0 = (s.y[0][...] - reaction(0)).astype(BF)

    def x0_block(k):
        return dot(w0, columns(s.v[0], 2 * k, 2), NN)

    def x0_give(k):
        both = x0_block(k).astype(BF)
        s.x0_out[k, 0] = both[:, :128]
        s.x0_out[k, 1] = both[:, 128:]
        remote(s.x0_out.at[k], s.x0_in.at[f], s.x0_send.at[k], s.x0_recv.at[f],
               dev(z, c, k)).start()

    def x0_maybe(k):
        to = plane(k)

        @pl.when(to < f)
        def _():
            x0_give(to)

    loop(0, 15, x0_maybe)
    mine = x0_block(f)
    s.x0_sum[0] = mine[:, :128]
    s.x0_sum[1] = mine[:, 128:]
    take_x(1)

    def x0_take(k):
        wait(s.x0_in.at[k], s.x0_recv.at[k])
        s.x0_sum[...] = s.x0_sum[...] + s.x0_in[k].astype(F32)

    loop(f + 1, FRONT, x0_take)
    for k in range(2):
        out[256 + k * 128:256 + (k + 1) * 128, :] = s.x0_sum[k].T
    give_x(1)

    loop(0, f, lambda k: wait(s.x0_out.at[k], s.x0_send.at[k]))
    loop(f + 1, FRONT, lambda k: wait(s.r.at[pl.ds(0, 2)], s.r_send.at[k]))
    wait(s.up_in[0], s.up_send[0])
    wait(s.g_half.at[0], s.g_swap.at[0])
    wait(s.g[3].at[f, pl.ds(0, 48)], s.gz.at[0])
    wait(s.g[0].at[pl.ds(0, 15)], s.g_send[0])
    for h in range(1, 5):
        n = 2 ** (h - 1)
        m = 256 >> h
        wait(s.v[h].at[pl.ds(0, 128)], s.v_fwd[h].at[0])
        if h < 4:
            wait(s.u[h].at[pl.ds(0, 128)], s.u_fwd[h].at[0])
        if n > 1:
            wait(s.v[h].at[pl.ds(0, (n - 1) * m)], s.v_send[h])
            if h < 4:
                wait(s.u[h].at[pl.ds(0, (n - 1) * m)], s.u_send[h])
            wait(s.zb[h].at[pl.ds(0, (n - 1) * m)], s.zb_send[h])
        away = jnp.int32(0)
        for zr in range(n):
            co, fo, _ = block_owner(h, zr)
            away = away + jnp.where(jnp.logical_and(co == c, fo == f), 0, 1)
        for count in range(max(n - 1, 1), n + 1):
            @pl.when(away == count)
            def _(count=count, h=h, m=m):
                wait(s.bn[h].at[pl.ds(0, count * m)], s.bn_send[h])
        wait(s.b[h].at[pl.ds(0, 30)], s.b_send[h])
        wait(s.b[h].at[0], s.b_swap[h].at[0])
        wait(s.vb[h].at[0, 0], s.swap[h].at[0])
        wait(s.sel_in[h], s.sel_send[h])
        if h > 1:
            wait(s.yz[h].at[pl.ds(1, 64 // SHARE[h] - 1)], s.yz_send[h])
        wait(s.vb[h].at[:, pl.ds(0, 15)], s.vb_send[h])
        wait(s.x_in[h], s.x_send[h])
        wait(s.x_sum[1].at[0] if h == 1 else s.x_sum[h], s.xx[h].at[0])
        if h < 4:
            wait(s.up_in[h], s.up_send[h])
            wait(s.g[h].at[pl.ds(0, 15)], s.g_send[h])


def hand_out(packed_rows, *refs):
    outs, sems = refs[:5], refs[5]
    copies = [pltpu.make_async_copy(packed_rows.at[pl.ds(256 >> h, 256 >> h)], outs[h].at[0, 0],
                                    sems.at[h]) for h in LEVELS]
    for copy in copies:
        copy.start()
    for copy in copies:
        copy.wait()


def on_device(*args):
    in_hbm = pl.BlockSpec(memory_space=pltpu.HBM)
    smem = pl.BlockSpec(memory_space=pltpu.SMEM)
    vmem = pl.BlockSpec(memory_space=pltpu.VMEM)
    packed_rows = pl.pallas_call(
        kernel,
        out_shape=jax.ShapeDtypeStruct((512, 128), F32),
        in_specs=[in_hbm] * 14 + [smem] * 4,
        out_specs=vmem,
        scratch_shapes=flat(scratch_shapes()),
        compiler_params=pltpu.CompilerParams(
            collective_id=0, has_side_effects=True, vmem_limit_bytes=56 * 2 ** 20),
        name="solve",
    )(*args)
    return tuple(pl.pallas_call(
        hand_out,
        out_shape=[jax.ShapeDtypeStruct(a.shape, F32) for a in args[:5]],
        in_specs=[vmem],
        out_specs=[in_hbm] * 5,
        scratch_shapes=[pltpu.SemaphoreType.DMA((5,))],
        name="hand_out",
    )(packed_rows))


def solution(mesh):
    shard = P("leaf", "front", None, None)
    return jax.shard_map(
        on_device,
        mesh=mesh,
        in_specs=(shard,) * 14 + (P(),) * 4,
        out_specs=(shard,) * 5,
        check_vma=False,
    )
```

```python
import types

import jax
import jax.numpy as jnp
from jax import lax
from jax.experimental import pallas as pl
from jax.experimental.pallas import tpu as pltpu
from jax.sharding import PartitionSpec as P

MESH = pl.DeviceIdType.MESH
BF = jnp.bfloat16
F32 = jnp.float32
NT = (((1,), (1,)), ((), ()))
NN = (((1,), (0,)), ((), ()))
FRONT = 16
LEVELS = range(5)
SHARE = (128, 64, 32, 16, 16)


def packed(numbers):
    return sum(n << 2 * i for i, n in enumerate(numbers))


STEPS = sorted(((dx, dy) for dx in range(4) for dy in range(4)),
               key=lambda s: -min(s[0], 4 - s[0]) - min(s[1], 4 - s[1]))
STEPS_X = packed(s[0] for s in STEPS[:15])
STEPS_Y = packed(s[1] for s in STEPS[:15])


def dot(a, b, dims):
    return lax.dot_general(a, b, dims, preferred_element_type=F32)


def side_by_side(parts):
    return jnp.concatenate(list(parts), axis=1)


def scratch_shapes():
    dma = pltpu.SemaphoreType.DMA

    def vm(*shape, dtype=BF):
        return pltpu.VMEM(shape, dtype)

    def per(make, levels):
        return [make(h) if h in levels else None for h in LEVELS]

    t = types.SimpleNamespace()
    low, high, every, lowered = range(0, 1), range(1, 5), range(0, 5), range(1, 4)
    t.v = per(lambda h: vm(256, 4096), every)
    t.u = per(lambda h: vm(256, 2048), range(0, 4))
    t.vblk = per(lambda h: vm(33, 256, 128), high)
    t.v_load = per(lambda h: dma(()), every)
    t.u_load = per(lambda h: dma(()), range(0, 4))
    t.v_send = per(lambda h: dma(()), range(2, 5))
    t.v_ring = dma((8,))
    t.u_send = per(lambda h: dma(()), range(2, 4))
    t.v_fwd = per(lambda h: dma((2,)), high)
    t.u_fwd = per(lambda h: dma((2,)), lowered)
    t.side = vm(256, 128)
    t.side_load = dma(())
    t.r = vm(32, 128, 128)
    t.r_send = dma((16,))
    t.r_recv = dma((16,))
    t.zb = per(lambda h: vm(128, 128), range(2, 5))
    t.zb_send = per(lambda h: dma(()), range(2, 5))
    t.zb_recv = per(lambda h: dma(()), range(2, 5))
    t.bn = per(lambda h: vm(128, 128), high)
    t.bn_send = per(lambda h: dma(()), high)
    t.bn_recv = per(lambda h: dma(()), high)
    t.bh = per(lambda h: vm(128 // SHARE[h], SHARE[h], 128), high)
    t.b = per(lambda h: vm(32, SHARE[h], 128), high)
    t.b_swap = per(lambda h: dma((2,)), high)
    t.b_send = per(lambda h: dma(()), high)
    t.b_recv = per(lambda h: dma(()), high)
    t.up_out = per(lambda h: vm(16, SHARE[h], 128), range(0, 4))
    t.up_in = per(lambda h: vm(15, SHARE[h], 128), range(0, 4))
    t.up_send = per(lambda h: dma(()), range(0, 4))
    t.up_recv = per(lambda h: dma(()), range(0, 4))
    t.halves = per(lambda h: vm(2, SHARE[h], 128), lowered)
    t.vb = per(lambda h: vm(2, 17, SHARE[h], 128), high)
    t.swap = per(lambda h: dma((2,)), high)
    t.vb_send = per(lambda h: dma(()), high)
    t.vb_recv = per(lambda h: dma((2, 16)), high)
    t.y = per(lambda h: vm(SHARE[h], 256, dtype=F32), range(0, 2))
    t.yz = per(lambda h: vm(64 // SHARE[h], SHARE[h], 256, dtype=F32), range(2, 5))
    t.yz_send = per(lambda h: dma(()), range(2, 5))
    t.yz_recv = per(lambda h: dma(()), range(2, 5))
    t.w = per(lambda h: vm(64, 256), high)
    t.w4 = vm(16, 256)
    t.sel_out = per(lambda h: vm(16, (0, 128, 64, 64, 16)[h], 128), high)
    t.sel_in = per(lambda h: vm(15, (0, 128, 64, 64, 16)[h], 128), high)
    t.gz = dma((2,))
    t.sel_send = per(lambda h: dma(()), high)
    t.sel_recv = per(lambda h: dma(()), high)
    t.g_half = vm(2, 64, 128)
    t.g_swap = dma((2,))
    t.g = per(lambda h: vm(16, 128, 128) if h == 0 else vm(17, 64, 128), range(0, 4))
    t.g_send = per(lambda h: dma(()), range(0, 4))
    t.g_recv = per(lambda h: dma((16,)), range(0, 4))
    t.x_out = per(lambda h: vm(2, 16, 64, 128) if h == 1 else vm(16, 256 >> h, 128), high)
    t.x_in = per(lambda h: vm(15, 2, 64, 128) if h == 1 else vm(15, 256 >> h, 128), high)
    t.x_send = per(lambda h: dma(()), high)
    t.x_recv = per(lambda h: dma(()), high)
    t.x_sum = per(lambda h: vm(2, 64, 128, dtype=F32) if h == 1 else vm(256 >> h, 128, dtype=F32), high)
    t.x_full = per(lambda h: vm(2, 64, 128, dtype=F32) if h == 1 else vm(256 >> h, 128, dtype=F32), high)
    t.xx = per(lambda h: dma((2,)), high)
    t.x0_out = vm(16, 2, 128, 128)
    t.x0_in = vm(16, 2, 128, 128)
    t.x0_sum = vm(2, 128, 128, dtype=F32)
    t.x0_send = dma((16,))
    t.x0_recv = dma((16,))
    return t


def flat(t):
    out = []
    for entry in vars(t).values():
        out += [e for e in entry if e is not None] if isinstance(entry, list) else [entry]
    return out


def unflat(t, refs):
    refs = iter(refs)
    s = types.SimpleNamespace()
    for name, entry in vars(t).items():
        if isinstance(entry, list):
            vars(s)[name] = [None if e is None else next(refs) for e in entry]
        else:
            vars(s)[name] = next(refs)
    return s


def kernel(*refs):
    sides = refs[0:5]
    invs = refs[5:10]
    lows = refs[10:14]
    maps = refs[14:18]
    out = refs[18]
    s = unflat(scratch_shapes(), refs[19:])

    leaf = lax.axis_index("leaf")
    f = lax.axis_index("front")
    z = leaf // 2
    c = leaf % 2
    other = 1 - c

    def dev(z_, c_, f_):
        return (2 * z_ + c_, f_)

    def remote(src, dst, send, recv, device):
        return pltpu.make_async_remote_copy(
            src_ref=src, dst_ref=dst, send_sem=send, recv_sem=recv,
            device_id=device, device_id_type=MESH)

    def wait(ref, sem):
        pltpu.make_async_copy(ref, ref, sem).wait()

    def loop(lo, hi, body):
        lax.fori_loop(lo, hi, lambda i, carry: (body(i), carry)[1], 0)

    fx, fy = f // 4, f % 4

    def step_of(k):
        if isinstance(k, int):
            return STEPS[k]
        return (STEPS_X >> 2 * k) % 4, (STEPS_Y >> 2 * k) % 4

    def plane(k):
        dx, dy = step_of(k)
        return (fx + dx) % 4 * 4 + (fy + dy) % 4

    def source(k):
        dx, dy = step_of(k)
        return (fx + 4 - dx) % 4 * 4 + (fy + 4 - dy) % 4

    def group(h):
        n = 2 ** (h - 1)
        zrel = z % n
        return n, zrel, z - zrel

    def share(h):
        return (0, 0, z % 2, z % 2 * 2 + z // 2 % 2, z % 2 * 2 + z // 2 % 2)[h]

    def own(ref):
        return ref.at[0, 0]

    def rows(first, count):
        return pl.ds(pl.multiple_of(first, count), count)

    def columns(ref, block, count=1):
        return ref[:, pl.ds(pl.multiple_of(block * 128, 128 * count), 128 * count)]

    side_copy = pltpu.make_async_copy(own(sides[0]), s.side, s.side_load)
    side_copy.start()
    barrier = pltpu.get_barrier_semaphore()

    def greet_plane(d):
        q = (c * FRONT + f + d) % (2 * FRONT)
        pl.semaphore_signal(barrier, inc=1, device_id=dev(z, q // FRONT, q % FRONT),
                            device_id_type=MESH)

    def greet_line(d):
        pl.semaphore_signal(barrier, inc=1, device_id=dev((z + d) % 8, c, f),
                            device_id_type=MESH)

    loop(1, 2 * FRONT, greet_plane)
    loop(1, 8, greet_line)
    load_v0 = pltpu.make_async_copy(own(invs[0]), s.v[0], s.v_load[0])
    load_u0 = pltpu.make_async_copy(own(lows[0]), s.u[0], s.u_load[0])
    load_v0.start()
    load_u0.start()
    for h in range(1, 5):
        n, zrel, _ = group(h)
        m = 256 >> h
        at = rows(c * 128 + zrel * m, m)
        pltpu.make_async_copy(own(invs[h]), s.v[h].at[at], s.v_load[h]).start()
        if h < 4:
            pltpu.make_async_copy(own(lows[h]), s.u[h].at[at], s.u_load[h]).start()
        if h > 1:
            pltpu.make_async_copy(own(sides[h]), s.zb[h].at[rows(zrel * m, m)], s.zb_recv[h]).start()
    side_copy.wait()
    for k in range(2):
        s.r[2 * f + k] = s.side[k * 128:(k + 1) * 128, :].astype(F32).T.astype(BF)
    for h in range(1, 5):
        s.vb[h][0, 16] = jnp.zeros((SHARE[h], 128), BF)
        s.vb[h][1, 16] = jnp.zeros((SHARE[h], 128), BF)
        s.vblk[h][32] = jnp.zeros((256, 128), BF)
        if h < 4:
            s.g[h][16] = jnp.zeros((64, 128), BF)
    pl.semaphore_wait(barrier, 31 + 7)

    def send_b0(k):
        to = plane(k)

        @pl.when(to > f)
        def _():
            mine = s.r.at[pl.ds(2 * f, 2)]
            remote(mine, mine, s.r_send.at[to], s.r_recv.at[f], dev(z, c, to)).start()

    loop(0, 15, send_b0)

    def block_owner(h, zr):
        n = 2 ** (h - 1)
        m = 256 >> h
        p = (2 * zr + c) * (32 >> h) + f // n
        return p % 2, p // 2, (f % n) * m

    def send_block_rows(h, src, zr):
        m = 256 >> h
        co, fo, row = block_owner(h, zr)
        dst = s.bn[h].at[rows(row, m)]
        here = jnp.logical_and(co == c, fo == f)

        @pl.when(here)
        def _():
            pltpu.make_async_copy(src, dst, s.bn_recv[h]).start()

        @pl.when(jnp.logical_not(here))
        def _():
            remote(src, dst, s.bn_send[h], s.bn_recv[h], dev(z, co, fo)).start()

    def gather_factor(h, ref, mine, send, load):
        n, zrel, zbase = group(h)
        m = 256 >> h
        dst = ref.at[rows(c * 128 + zrel * m, m)]
        for d in range(1, n):
            remote(own(mine), dst, send, load, dev(zbase + (zrel + d) % n, c, f)).start()

    def gather_level(h):
        gather_factor(h, s.v[h], invs[h], s.v_send[h], s.v_load[h])
        gather_factor(h, s.u[h], lows[h], s.u_send[h], s.u_load[h])

    def forward_factor(ref, load, fwd):
        part = ref.at[rows(c * 128, 128)]
        if load is not None:
            wait(part, load)
        remote(part, part, fwd.at[0], fwd.at[1], dev(z, other, f)).start()

    def ring(step):
        def rows_of(d):
            return s.v[4].at[rows(c * 128 + (z + 8 + d) % 8 * 16, 16)]

        def pass_on(d, to):
            remote(rows_of(d), rows_of(d), s.v_send[4], s.v_ring.at[(z + 8 + d) % 8],
                   dev((z + 8 + to) % 8, c, f)).start()

        def arrived(d):
            wait(rows_of(d), s.v_ring.at[(z + 8 + d) % 8])

        if step == 1:
            wait(rows_of(0), s.v_load[4])
            pass_on(0, 1)
            pass_on(0, -1)
        elif step < 4:
            arrived(1 - step)
            pass_on(1 - step, 1)
            arrived(step - 1)
            pass_on(step - 1, -1)
        elif step == 4:
            arrived(-3)
            pass_on(-3, 1)
        else:
            arrived(3)
            arrived(-4)

    def forward_level(h):
        forward_factor(s.v[h], s.v_load[h] if h < 4 else None, s.v_fwd[h])
        if h < 4:
            forward_factor(s.u[h], s.u_load[h], s.u_fwd[h])

    def have_forward(ref, fwd):
        wait(ref.at[rows(other * 128, 128)], fwd.at[1])

    send_block_rows(1, own(sides[1]), 0)
    for h in range(2, 5):
        n, zrel, zbase = group(h)
        m = 256 >> h
        for d in range(1, n):
            remote(own(sides[h]), s.zb[h].at[rows(zrel * m, m)], s.zb_send[h], s.zb_recv[h],
                   dev(zbase + (zrel + d) % n, c, f)).start()
    gather_level(2)
    gather_level(3)
    forward_level(1)

    load_v0.wait()

    def y0_term(k):
        return dot(side_by_side([s.r[2 * k], s.r[2 * k + 1]]), columns(s.v[0], 2 * k, 2), NT)

    def y0_step(d, acc):
        k = f - d
        wait(s.r.at[pl.ds(0, 2)], s.r_recv.at[k])
        return acc + y0_term(k)

    y0 = lax.fori_loop(1, f + 1, y0_step, y0_term(f))
    s.y[0][...] = y0
    y0 = y0.astype(BF)
    load_u0.wait()

    def by_fours(body):
        loop(0, 3, lambda q: body([4 * q, 4 * q + 1, 4 * q + 2, 4 * q + 3]))
        body([12, 13, 14, 15])

    def here(k):
        return isinstance(k, int) and k == 15

    def up(h, y):
        def four(ks):
            part = dot(y, side_by_side(columns(s.u[h], plane(k)) for k in ks), NN).astype(BF)
            for n, k in enumerate(ks):
                i = plane(k)
                s.up_out[h][i] = part[:, n * 128:(n + 1) * 128]
                if not here(k):
                    remote(s.up_out[h].at[i], s.up_in[h].at[k], s.up_send[h], s.up_recv[h],
                           dev(z, c, i)).start()

        by_fours(four)

    up(0, y0)

    def turn_b(h):
        wait(s.bn[h], s.bn_recv[h])
        turned = s.bn[h][...].astype(F32).T.astype(BF)
        s.bh[h][...] = turned.reshape(s.bh[h].shape)
        block = 2 * f + c
        shares = 64 // SHARE[h]
        s.b[h][block] = s.bh[h][c * shares + share(h)]
        remote(s.bh[h].at[other * shares + share(h)], s.b[h].at[block], s.b_swap[h].at[0],
               s.b_swap[h].at[1], dev(z, other, f)).start()

    def spread_b(h):
        wait(s.b[h].at[0], s.b_swap[h].at[1])
        both = s.b[h].at[pl.ds(2 * f, 2)]
        loop(0, 15, lambda k: remote(both, both, s.b_send[h], s.b_recv[h],
                                     dev(z, c, plane(k))).start())

    def split_columns(h):
        have_forward(s.v[h], s.v_fwd[h])

        def one(k):
            s.vblk[h][k] = columns(s.v[h], k)

        loop(0, 32, one)

    turn_b(1)
    for h in range(2, 5):
        m = 256 >> h
        wait(s.zb[h], s.zb_recv[h])
        for zr in range(2 ** (h - 1)):
            send_block_rows(h, s.zb[h].at[pl.ds(zr * m, m)], zr)
    split_columns(1)
    spread_b(1)

    def send_child(h, child, kind):
        at = s.vb[h].at[child, f]
        loop(0, 15, lambda k: remote(at, at, s.vb_send[h], s.vb_recv[h].at[kind, f],
                                     dev(z, c, plane(k))).start())

    def side_term(h):
        wait(s.b[h].at[pl.ds(0, 30)], s.b_recv[h])

        def step(j, acc):
            part = side_by_side(s.b[h][8 * j + k] for k in range(8))
            return acc + dot(part, columns(s.v[h], 8 * j, 8), NT)

        return lax.fori_loop(0, 4, step, jnp.zeros((SHARE[h], 256), F32))

    def child_term(h, child, kind, acc):
        table = maps[h - 1]
        row = 2 * (z // 2 ** (h - 1)) + child

        def pair(ks):
            at = [jnp.minimum(table[row, k], 32) for k in ks]
            return dot(side_by_side(s.vb[h][child, k] for k in ks),
                       side_by_side(s.vblk[h][a] for a in at), NT)

        def arrived(k):
            wait(s.vb[h].at[0, 0], s.vb_recv[h].at[kind, source(k)])

        def step(q, acc):
            arrived(14 - 2 * q)
            arrived(13 - 2 * q)
            return acc - pair([source(14 - 2 * q), source(13 - 2 * q)])

        acc = lax.fori_loop(0, 7, step, acc)
        arrived(0)
        return acc - pair([f, source(0)])

    def bottom_block(h, child):
        table = maps[h - 1]
        row = 2 * (z // 2 ** (h - 1)) + child
        less = jnp.int32(0)
        hit = jnp.int32(0)
        for i in range(16):
            less = less + (table[row, i] < 32 + f).astype(jnp.int32)
            hit = hit + (table[row, i] == 32 + f).astype(jnp.int32)
        return jnp.where(hit > 0, less, 16)

    def summed(ref, first):
        total = first
        for k in range(15):
            total = total + ref[k].astype(F32)
        return total

    def give_blocks(h, mine, half, sibling):
        remote(half, s.vb[h].at[mine, f], s.swap[h].at[0], s.swap[h].at[1], sibling).start()
        send_child(h, mine, 0)
        wait(s.vb[h].at[mine, f], s.swap[h].at[1])
        send_child(h, 1 - mine, 1)

    wait(s.up_in[0], s.up_recv[0])
    total = summed(s.up_in[0], s.up_out[0][f].astype(F32)).astype(BF)
    s.halves[1][...] = total.reshape(2, 64, 128)
    s.vb[1][c, f] = s.halves[1][c]
    give_blocks(1, c, s.halves[1].at[other], dev(z, other, f))
    for h in range(2, 5):
        turn_b(h)

    for h in range(1, 5):
        mine = c if h == 1 else z // 2 ** (h - 2) % 2
        acc = side_term(h)
        acc = child_term(h, mine, 0, acc)
        acc = child_term(h, 1 - mine, 1, acc)
        y = acc.astype(BF)
        if h == 1:
            s.y[1][...] = acc
        else:
            n = 64 // SHARE[h]
            mine = s.yz[h].at[share(h)]
            s.yz[h][share(h)] = acc
            for d in range(1, n):
                remote(mine, mine, s.yz_send[h], s.yz_recv[h],
                       dev(z - z % n + (z + d) % n, c, f)).start()
        if h == 4:
            s.w4[...] = y
            break
        have_forward(s.u[h], s.u_fwd[h])
        up(h, y)
        spread_b(h + 1)
        if h < 3:
            forward_level(h + 1)
        if h > 1:
            ring(2 * h - 2)
        bottom = [bottom_block(h, child) for child in range(2)]
        if h < 3:
            split_columns(h + 1)
        kept = s.vb[h][0, bottom[0]].astype(F32) + s.vb[h][1, bottom[1]].astype(F32)
        kept = kept + s.up_out[h][f].astype(F32)
        wait(s.up_in[h], s.up_recv[h])
        step = 2 ** (h - 1)
        mine = z // step % 2
        total = summed(s.up_in[h], kept).astype(BF)
        if h < 3:
            s.halves[h + 1][...] = total.reshape(s.halves[h + 1].shape)
            s.vb[h + 1][mine, f] = s.halves[h + 1][mine]
            half = s.halves[h + 1].at[1 - mine]
        else:
            s.vb[4][mine, f] = total
            half = s.vb[4].at[mine, f]
        give_blocks(h + 1, mine, half, dev(z + step - 2 * step * mine, c, f))
        if h < 3:
            ring(2 * h - 1)
        else:
            ring(5)
            forward_level(4)
            split_columns(4)

    def take_x(h):
        wait(s.x_in[h], s.x_recv[h])
        if h == 1:
            s.x_sum[1][...] = summed(s.x_in[1], s.x_out[1][:, f].astype(F32))
            s.x_full[1][c] = s.x_sum[1][c]
            src, dst = s.x_sum[1].at[other], s.x_full[1].at[c]
        else:
            s.x_sum[h][...] = summed(s.x_in[h], s.x_out[h][f].astype(F32))
            src, dst = s.x_sum[h], s.x_full[h]
        remote(src, dst, s.xx[h].at[0], s.xx[h].at[1], dev(z, other, f)).start()

    def give_x(h):
        m = 256 >> h
        if h == 1:
            wait(s.x_full[1].at[0], s.xx[1].at[1])
            out[m:2 * m, :] = s.x_full[1][...].reshape(128, 128).T
        else:
            wait(s.x_full[h], s.xx[h].at[1])
            theirs = s.x_full[h][...]
            theirs = side_by_side([theirs[:, 64:], theirs[:, :64]])
            lane = lax.broadcasted_iota(jnp.int32, (m, 128), 1)
            out[m:2 * m, :] = jnp.where(lane // 64 == c, s.x_sum[h][...], theirs)

    def reaction(h):
        def pair(ks):
            return dot(side_by_side(s.g[h][k] for k in ks),
                       side_by_side(columns(s.u[h], k) for k in ks), NT)

        def arrived(k):
            wait(s.g[h].at[0], s.g_recv[h].at[source(k)])

        def step(q, acc):
            arrived(14 - 2 * q)
            arrived(13 - 2 * q)
            return acc + pair([source(14 - 2 * q), source(13 - 2 * q)])

        acc = lax.fori_loop(0, 7, step, jnp.zeros((128 if h == 0 else 64, 256), F32))
        arrived(0)
        return acc + pair([f, source(0)])

    def send_rows(h):
        _, zrel, _ = group(h)
        half = 32 >> h
        first = zrel * 2 * half
        w = s.w[h][...]
        if h == 1:
            for part in range(2):
                def x_step(q, part=part):
                    both = dot(w, columns(s.v[1], first + part * half + 2 * q, 2), NN).astype(BF)
                    s.x_out[1][part, 2 * q] = both[:, :128]
                    s.x_out[1][part, 2 * q + 1] = both[:, 128:]

                loop(0, half // 2, x_step)
        else:
            m = 256 >> h

            def row_step(q):
                both = [dot(w, columns(s.v[h], first + part * half + q), NN) for part in range(2)]
                turned = jnp.concatenate(both, axis=0).T.astype(BF)
                s.x_out[h][pl.ds(q * (128 // m), 128 // m)] = turned.reshape(128 // m, m, 128)

            loop(0, half, row_step)

        def send(k):
            src = s.x_out[1].at[:, plane(k)] if h == 1 else s.x_out[h].at[plane(k)]
            remote(src, s.x_in[h].at[k], s.x_send[h], s.x_recv[h], dev(z, c, plane(k))).start()

        loop(0, 15, send)

    def send_g(h):
        at = s.g[h].at[f]
        loop(0, 15, lambda k: remote(at, at, s.g_send[h], s.g_recv[h].at[f],
                                     dev(z, c, plane(k))).start())

    for h in range(4, 0, -1):
        if h == 1:
            s.w[1][...] = (s.y[1][...] - reaction(1)).astype(BF)
        elif h < 4:
            react = reaction(h)
            wait(s.yz[h].at[pl.ds(1, 64 // SHARE[h] - 1)], s.yz_recv[h])
            s.w[h][...] = (s.yz[h][...].reshape(64, 256) - react).astype(BF)
        w_sel = s.w4 if h == 4 else s.w[h]
        table = maps[h - 1]
        first = 2 * z if h == 1 else z // 2 ** (h - 2)

        def select(ks, child, h=h, table=table, first=first, w_sel=w_sel):
            at = [table[first + child, plane(k)] for k in ks]
            part = dot(w_sel[...], side_by_side(s.vblk[h][jnp.minimum(a, 32)] for a in at), NN)
            blocks = [part[:, n * 128:(n + 1) * 128] for n in range(4)]
            if here(ks[3]) and h < 4:
                kept = jnp.where(at[3] >= 32, at[3] - 32, 16)
                blocks[3] = blocks[3] + s.g[h][kept].astype(F32)
            return blocks

        def down(ks, h=h, select=select):
            for child in range(2 if h == 1 else 1):
                for k, block in zip(ks, select(ks, child)):
                    n = block.shape[0]
                    s.sel_out[h][plane(k), child * n:(child + 1) * n] = block.astype(BF)
            for k in ks:
                i = plane(k)
                if not here(k):
                    remote(s.sel_out[h].at[i], s.sel_in[h].at[k], s.sel_send[h], s.sel_recv[h],
                           dev(z, c, i)).start()

        by_fours(down)

        if h < 4:
            take_x(h + 1)

        wait(s.sel_in[h], s.sel_recv[h])
        total = summed(s.sel_in[h], s.sel_out[h][f].astype(F32)).astype(BF)
        if h == 4:
            mine = s.g[3].at[f, rows(share(4) * 16, 16)]
            s.g[3][f, rows(share(4) * 16, 16)] = total
            for d in range(1, 4):
                remote(mine, mine, s.gz.at[0], s.gz.at[1], dev(z - z % 4 + (z + d) % 4, c, f)).start()
            wait(s.g[3].at[f, pl.ds(0, 48)], s.gz.at[1])
        elif h > 1:
            s.g[h - 1][f] = total
        else:
            s.g_half[0] = total[:64]
            s.g_half[1] = total[64:]
            half = s.g[0].at[f, rows(c * 64, 64)]
            s.g[0][f, rows(c * 64, 64)] = s.g_half[c]
            remote(s.g_half.at[other], half, s.g_swap.at[0], s.g_swap.at[1],
                   dev(z, other, f)).start()
            wait(half, s.g_swap.at[1])
        send_g(h - 1)
        if h < 4:
            send_rows(h)
            give_x(h + 1)
        else:
            wait(s.yz[4].at[pl.ds(1, 3)], s.yz_recv[4])
            s.w[4][...] = s.yz[4][...].reshape(64, 256).astype(BF)
            send_rows(4)

    w0 = (s.y[0][...] - reaction(0)).astype(BF)

    def x0_block(k):
        return dot(w0, columns(s.v[0], 2 * k, 2), NN)

    def x0_give(k):
        both = x0_block(k).astype(BF)
        s.x0_out[k, 0] = both[:, :128]
        s.x0_out[k, 1] = both[:, 128:]
        remote(s.x0_out.at[k], s.x0_in.at[f], s.x0_send.at[k], s.x0_recv.at[f],
               dev(z, c, k)).start()

    def x0_maybe(k):
        to = plane(k)

        @pl.when(to < f)
        def _():
            x0_give(to)

    loop(0, 15, x0_maybe)
    mine = x0_block(f)
    s.x0_sum[0] = mine[:, :128]
    s.x0_sum[1] = mine[:, 128:]
    take_x(1)

    def x0_take(k):
        wait(s.x0_in.at[k], s.x0_recv.at[k])
        s.x0_sum[...] = s.x0_sum[...] + s.x0_in[k].astype(F32)

    give_x(1)
    loop(f + 1, FRONT, x0_take)
    for k in range(2):
        out[256 + k * 128:256 + (k + 1) * 128, :] = s.x0_sum[k].T

    loop(0, f, lambda k: wait(s.x0_out.at[k], s.x0_send.at[k]))
    loop(f + 1, FRONT, lambda k: wait(s.r.at[pl.ds(0, 2)], s.r_send.at[k]))
    wait(s.up_in[0], s.up_send[0])
    wait(s.g_half.at[0], s.g_swap.at[0])
    wait(s.g[3].at[f, pl.ds(0, 48)], s.gz.at[0])
    wait(s.g[0].at[pl.ds(0, 15)], s.g_send[0])
    for h in range(1, 5):
        n = 2 ** (h - 1)
        m = 256 >> h
        wait(s.v[h].at[pl.ds(0, 128)], s.v_fwd[h].at[0])
        if h < 4:
            wait(s.u[h].at[pl.ds(0, 128)], s.u_fwd[h].at[0])
        if n > 1:
            wait(s.v[h].at[pl.ds(0, (n - 1) * m)], s.v_send[h])
            if h < 4:
                wait(s.u[h].at[pl.ds(0, (n - 1) * m)], s.u_send[h])
            wait(s.zb[h].at[pl.ds(0, (n - 1) * m)], s.zb_send[h])
        away = jnp.int32(0)
        for zr in range(n):
            co, fo, _ = block_owner(h, zr)
            away = away + jnp.where(jnp.logical_and(co == c, fo == f), 0, 1)
        for count in range(max(n - 1, 1), n + 1):
            @pl.when(away == count)
            def _(count=count, h=h, m=m):
                wait(s.bn[h].at[pl.ds(0, count * m)], s.bn_send[h])
        wait(s.b[h].at[pl.ds(0, 30)], s.b_send[h])
        wait(s.b[h].at[0], s.b_swap[h].at[0])
        wait(s.vb[h].at[0, 0], s.swap[h].at[0])
        wait(s.sel_in[h], s.sel_send[h])
        if h > 1:
            wait(s.yz[h].at[pl.ds(1, 64 // SHARE[h] - 1)], s.yz_send[h])
        wait(s.vb[h].at[:, pl.ds(0, 15)], s.vb_send[h])
        wait(s.x_in[h], s.x_send[h])
        wait(s.x_sum[1].at[0] if h == 1 else s.x_sum[h], s.xx[h].at[0])
        if h < 4:
            wait(s.up_in[h], s.up_send[h])
            wait(s.g[h].at[pl.ds(0, 15)], s.g_send[h])


def hand_out(packed_rows, *refs):
    outs, sems = refs[:5], refs[5]
    copies = [pltpu.make_async_copy(packed_rows.at[pl.ds(256 >> h, 256 >> h)], outs[h].at[0, 0],
                                    sems.at[h]) for h in LEVELS]
    for copy in copies:
        copy.start()
    for copy in copies:
        copy.wait()


def on_device(*args):
    in_hbm = pl.BlockSpec(memory_space=pltpu.HBM)
    smem = pl.BlockSpec(memory_space=pltpu.SMEM)
    vmem = pl.BlockSpec(memory_space=pltpu.VMEM)
    packed_rows = pl.pallas_call(
        kernel,
        out_shape=jax.ShapeDtypeStruct((512, 128), F32),
        in_specs=[in_hbm] * 14 + [smem] * 4,
        out_specs=vmem,
        scratch_shapes=flat(scratch_shapes()),
        compiler_params=pltpu.CompilerParams(
            collective_id=0, has_side_effects=True, vmem_limit_bytes=56 * 2 ** 20),
        name="solve",
    )(*args)
    return tuple(pl.pallas_call(
        hand_out,
        out_shape=[jax.ShapeDtypeStruct(a.shape, F32) for a in args[:5]],
        in_specs=[vmem],
        out_specs=[in_hbm] * 5,
        scratch_shapes=[pltpu.SemaphoreType.DMA((5,))],
        name="hand_out",
    )(packed_rows))


def solution(mesh):
    shard = P("leaf", "front", None, None)
    return jax.shard_map(
        on_device,
        mesh=mesh,
        in_specs=(shard,) * 14 + (P(),) * 4,
        out_specs=(shard,) * 5,
        check_vma=False,
    )
```
